256 devices in a mesh: band: 16 (over y_hi, z), space: 16 (over y_lo, x, core).
Axes of the slice: x: 4, y: 4 (y_hi: 2, y_lo: 2; y = y_hi * 2 + y_lo), z: 8, core: 2. Of those that a mesh axis runs over, the one named last changes fastest.
Arguments:
- psi_start: float32 [2, 32, 16, 9216], P(None, 'band', 'space'), may hold values from -6 to 6
- adjoint_end: float32 [2, 32, 16, 9216], P(None, 'band', 'space'), may hold values from -6 to 6
- potential_now: float32 [16, 9216], P('space'), may hold values from -12 to 12
- potential_next: float32 [16, 9216], P('space'), may hold values from -12 to 12
- projector_tiles: float32 [16, 16, 9216], P('band', 'space'), may hold values from -0.015625 to 0.015625
- tile_map: int32 [4, 16, 72], P(None, 'space'), may hold values 0 or 1
- strengths: float32 [16], replicated, may hold values from 30 to 90
- positions: int32 [3, 4], replicated, may hold values from 0 to 95, as said below
Outputs:
- psi_end: float32 [2, 32, 16, 9216], P(None, 'band', 'space')
- adjoint_start: float32 [2, 32, 16, 9216], P(None, 'band', 'space')
- adjoint_density: float32 [16, 9216], P('space', 'band')
- forces: float32 [3, 4], replicated
The draws below stay inside these ranges and needn't reach their ends.
Inputs may be any that keep to these rules, and one draw needn't show every extreme that they name: positions[0], positions[1], positions[2] hold an atom's plane, row and column, within 0 to 15, 95 and 95.
All inputs are finite; a program needn't handle non-finite values. No bound on the sum of `tile_map` on one device may be relied on, other than what follows from the above.
Results may differ from the reference program's by a relative error of at most 0.00016.
Values sent between devices are 32-bit elements; how exact they have to be, the bound alone decides.
No kernel may reach another device: no remote copies, remote signals or barrier semaphores. Data moves between devices by JAX's collectives and lax.ppermute only.
A program may use at most 128 MiB of HBM per device.

```python
import math
import jax
import jax.numpy as jnp
from jax import lax

NB = 32
NY = 96
NZ = 96
ATOMS = 4
PRJ_ATOM = 4
NX = 16
NYZ = 9216
TILES = 72
NPRJ = 16


def draw_positions(key, part):
    key = jax.random.fold_in(key, 7)
    key_x, key_y, key_z = jax.random.split(key, 3)
    along_x = jax.random.randint(key_x, (ATOMS,), 0, NX)
    along_y = jax.random.randint(key_y, (ATOMS,), 0, NY)
    along_z = jax.random.randint(key_z, (ATOMS,), 0, NZ)
    along_x = along_x.at[0].set(NX - 1)
    along_z = along_z.at[0].set(NZ - 1)
    along_y = along_y.at[1].set(0)
    return jnp.stack([along_x, along_y, along_z]).astype(jnp.int32)


def touch_ends(values, own_key, smallest, high):
    spot = [jax.random.randint(jax.random.fold_in(own_key, axis), (), 0, length) for axis, length in enumerate(values.shape)]
    main_axis = values.shape.index(max(values.shape))
    neighbour = spot[:main_axis] + [(spot[main_axis] + 1) % values.shape[main_axis]] + spot[main_axis + 1:]
    return values.at[tuple(spot)].set(smallest).at[tuple(neighbour)].set(high)


def block_scale(rng, shape, cuts, smallest, high):
    gain, own = 1.0, jax.random.fold_in(rng, 6)
    for position, shards_of in cuts:
        draws = jnp.exp(jax.random.uniform(jax.random.fold_in(own, position), (shards_of,), jnp.float32, smallest / len(cuts), high / len(cuts)))
        gain = gain * jnp.repeat(draws, shape[position] // shards_of).reshape([-1 if axis == position else 1 for axis in range(len(shape))])
    return gain


def normal_values(rng, dims, deviation, reach, cuts=(), held_as=jnp.bfloat16):
    result = deviation * jax.random.normal(rng, dims, jnp.float32)
    if cuts:
        result = result * block_scale(rng, dims, cuts, -0.22, 0.18)
    return jnp.clip(result, -reach, reach).astype(held_as)


def setup_inputs(seed: int = 0) -> dict:
    seeds = jax.random.split(jax.random.key(seed), 9)
    psi_start = normal_values(seeds[0], (2, NB, NX, NYZ), 1.0, 6.0, ((1, 16), (2, 16)), jnp.float32)
    adjoint_end = normal_values(seeds[1], (2, NB, NX, NYZ), 1.0, 6.0, ((1, 16), (2, 16)), jnp.float32)
    potential_now = normal_values(seeds[2], (NX, NYZ), 3.0, 12.0, ((0, 16),), jnp.float32)
    potential_next = normal_values(seeds[3], (NX, NYZ), 3.0, 12.0, ((0, 16),), jnp.float32)
    projector_tiles = normal_values(seeds[4], (NPRJ, NX, NYZ), (NX * NYZ) ** -0.5, 0.015625, ((0, 16), (1, 16)), jnp.float32)
    tile_map = touch_ends((jax.random.randint(seeds[5], (ATOMS, NX, TILES), 0, 3) < 1).astype(jnp.int32), jax.random.fold_in(seeds[5], 1), 0, 1)
    strengths = jnp.clip(jnp.exp(jax.random.uniform(seeds[6], (NPRJ,), jnp.float32, math.log(30.0), math.log(90.0))), 30.0, 90.0)
    positions = draw_positions(jax.random.fold_in(seeds[8], 71), 0)
    return {"psi_start": psi_start, "adjoint_end": adjoint_end, "potential_now": potential_now, "potential_next": potential_next, "projector_tiles": projector_tiles, "tile_map": tile_map, "strengths": strengths, "positions": positions}


half_step = 0.025
kinetic_scale = 3.125
highest = lax.Precision.HIGHEST


def projectors(projector_tiles, tile_map, positions):
    shaped = projector_tiles.reshape(ATOMS, PRJ_ATOM, NX, TILES, 128)
    masked = shaped * tile_map.astype(jnp.float32).reshape(ATOMS, 1, NX, TILES, 1)
    beta = masked.reshape(ATOMS, PRJ_ATOM, NX, NY, NZ)
    plane_index = jnp.arange(NX, dtype=jnp.int32)
    row_index = jnp.arange(NY, dtype=jnp.int32)
    column = jnp.arange(NZ, dtype=jnp.int32)
    wave_x = jnp.sin((2.0 * math.pi / NX) * (plane_index[None, :] - positions[0][:, None]).astype(jnp.float32))
    wave_y = jnp.sin((2.0 * math.pi / NY) * (row_index[None, :] - positions[1][:, None]).astype(jnp.float32))
    wave_z = jnp.sin((2.0 * math.pi / NZ) * (column[None, :] - positions[2][:, None]).astype(jnp.float32))
    slope_x = beta * wave_x[:, None, :, None, None]
    slope_y = beta * wave_y[:, None, None, :, None]
    slope_z = beta * wave_z[:, None, None, None, :]
    grid_points = NX * NYZ
    return jnp.concatenate([beta.reshape(NPRJ, grid_points), slope_x.reshape(NPRJ, grid_points),
                            slope_y.reshape(NPRJ, grid_points), slope_z.reshape(NPRJ, grid_points)], 0)


def hamiltonian(fields, potential, basis_rows, strengths):
    field_grid = fields.reshape(fields.shape[:-1] + (NY, NZ))
    beside_all = jnp.roll(field_grid, -1, 2) + jnp.roll(field_grid, 1, 2)
    beside_all = beside_all + jnp.roll(field_grid, -1, 3) + jnp.roll(field_grid, 1, 3)
    beside_all = beside_all + jnp.roll(field_grid, -1, 4) + jnp.roll(field_grid, 1, 4)
    beside_all = beside_all.reshape(fields.shape)
    flat_rows = fields.reshape(-1, NX * NYZ)
    coeffs = jnp.dot(flat_rows, basis_rows.T, precision=highest, preferred_element_type=jnp.float32)
    projected = jnp.dot(coeffs * strengths, basis_rows, precision=highest,
                        preferred_element_type=jnp.float32).reshape(fields.shape)
    return kinetic_scale * (6.0 * fields - beside_all) + potential * fields + projected


def taylor(fields, potential, direction, basis_rows, strengths):
    accumulated = fields
    current = fields
    for degree in range(1, 5):
        applied = hamiltonian(current, potential, basis_rows, strengths)
        factor = direction * half_step / degree
        current = jnp.stack([-(factor * applied[1]), factor * applied[0]])
        accumulated = accumulated + current
    return accumulated


def reference(psi_start, adjoint_end, potential_now, potential_next, projector_tiles, tile_map, strengths, positions):
    extended = projectors(projector_tiles, tile_map, positions)
    basis_rows = extended[:NPRJ]
    block_width = 32
    block_count = NB // block_width

    def propagate_block(carried, incoming):
        density, force = carried
        orbital, adjoint = incoming
        psi_half = taylor(orbital, potential_now, -1.0, basis_rows, strengths)
        adjoint_half = taylor(adjoint, potential_next, 1.0, basis_rows, strengths)
        psi_end = taylor(psi_half, potential_next, -1.0, basis_rows, strengths)
        adjoint_start = taylor(adjoint_half, potential_now, 1.0, basis_rows, strengths)
        density = density + (2.0 * half_step) * jnp.sum(psi_half[0] * adjoint_half[1] - psi_half[1] * adjoint_half[0], axis=0)
        coeff_psi = jnp.dot(psi_half.reshape(-1, NX * NYZ), extended.T, precision=highest,
                            preferred_element_type=jnp.float32).reshape(2, block_width, 4, NPRJ)
        coeff_adj = jnp.dot(adjoint_half.reshape(-1, NX * NYZ), extended.T, precision=highest,
                            preferred_element_type=jnp.float32).reshape(2, block_width, 4, NPRJ)
        products = coeff_psi[:, :, :1] * coeff_adj[:, :, 1:] + coeff_adj[:, :, :1] * coeff_psi[:, :, 1:]
        weighted = jnp.sum(products, axis=(0, 1)) * strengths
        force = force + jnp.sum(weighted.reshape(3, ATOMS, PRJ_ATOM), axis=2)
        return (density, force), (psi_end, adjoint_start)

    orbital_blocks = psi_start.reshape(2, block_count, block_width, NX, NYZ).transpose(1, 0, 2, 3, 4)
    adjoint_blocks = adjoint_end.reshape(2, block_count, block_width, NX, NYZ).transpose(1, 0, 2, 3, 4)
    initial = (jnp.zeros((NX, NYZ), jnp.float32), jnp.zeros((3, ATOMS), jnp.float32))
    (density, force), (ends, starts) = lax.scan(propagate_block, initial, (orbital_blocks, adjoint_blocks))
    psi_end = ends.transpose(1, 0, 2, 3, 4).reshape(2, NB, NX, NYZ)
    adjoint_start = starts.transpose(1, 0, 2, 3, 4).reshape(2, NB, NX, NYZ)
    return psi_end, adjoint_start, density, force / NB
```

```python
import functools
import math

import jax
import jax.numpy as jnp
import numpy as np
from jax import lax
from jax.experimental import pallas as pl
from jax.experimental.pallas import tpu as pltpu
from jax.sharding import PartitionSpec as P

NB = 32
NY = 96
NZ = 96
ROWS = 72
LANES = 128
PRJ = 16
PRJ_ATOM = 4

half_step = 0.025
kinetic_scale = 3.125
highest = lax.Precision.HIGHEST
f32 = jnp.float32

A2 = -(half_step**2) / 2.0
A3 = -(half_step**3) / 6.0
A4 = half_step**4 / 24.0


def neighbour_masks():
    flat = np.arange(ROWS * LANES)
    lane, column = flat % LANES, flat % NZ
    masks = [
        (column == 95) & (lane >= 95),
        (column != 95) & (lane < 127),
        (column == 0) & (lane < 33),
        (column != 0) & (lane >= 1),
        (column == 32) & (lane >= 33),
        (column != 31) & (lane == 127),
        (column == 63) & (lane < 95),
        (column != 64) & (lane == 0),
    ]
    return np.stack(masks).astype(np.float32).reshape(8, ROWS, LANES)


def in_plane(x, masks):
    lane = lax.broadcasted_iota(jnp.int32, (ROWS, LANES), 1)
    up_z = pltpu.roll(x, 127, 1)
    up_z_end = pltpu.roll(x, 95, 1)
    down_z = pltpu.roll(x, 1, 1)
    down_z_end = pltpu.roll(x, 33, 1)
    up_y = pltpu.roll(x, 32, 1)
    down_y = pltpu.roll(x, 96, 1)
    same = (
        masks[0] * up_z_end
        + masks[1] * up_z
        + masks[2] * down_z_end
        + masks[3] * down_z
        + jnp.where(lane < 32, up_y, 0.0)
        + jnp.where(lane >= 96, down_y, 0.0)
    )
    after = masks[4] * down_z_end + masks[5] * up_z + jnp.where(lane >= 32, up_y, 0.0)
    before = masks[6] * up_z_end + masks[7] * down_z + jnp.where(lane < 96, down_y, 0.0)
    return same + pltpu.roll(after, ROWS - 1, 0) + pltpu.roll(before, 1, 0)


def local(x, beside, potential, masks):
    return kinetic_scale * (6.0 * x - in_plane(x, masks) - beside) + potential * x


def fold(x):
    return jnp.sum(x.reshape(ROWS // 8, 8, LANES), axis=0)


def rows8(parts):
    sub = lax.broadcasted_iota(jnp.int32, (8, LANES), 0)
    low = sub < 4
    parts = [
        jnp.where(low, a, b) + pltpu.roll(jnp.where(low, b, a), 4, 0)
        for a, b in zip(parts[:4], parts[4:])
    ]
    for step in (2, 1):
        first = (sub & step) == 0
        parts = [
            jnp.where(first, a + pltpu.roll(a, 8 - step, 0), b + pltpu.roll(b, step, 0))
            for a, b in zip(parts[:step], parts[step:])
        ]
    return parts[0]


def params(mib):
    return pltpu.CompilerParams(vmem_limit_bytes=mib * 2**20)


VMEM = pl.BlockSpec(memory_space=pltpu.VMEM)
SMEM = pl.BlockSpec(memory_space=pltpu.SMEM)


def call(kernel, outs, args, scratch=(), scalars=0, mib=24, cost=None):
    specs = [SMEM] * scalars + [VMEM] * (len(args) - scalars)
    single = not isinstance(outs, list)
    shapes = [jax.ShapeDtypeStruct(o, f32) for o in ([outs] if single else outs)]
    result = pl.pallas_call(
        kernel,
        out_shape=shapes,
        in_specs=specs,
        out_specs=[VMEM] * len(shapes),
        scratch_shapes=list(scratch),
        compiler_params=params(mib),
        cost_estimate=cost,
    )(*args)
    return result[0] if single else result


def projector_kernel(beta, beside_a, beside_b, masks, out):
    x = beta[...]
    out[0] = x
    out[1] = kinetic_scale * (6.0 * x - in_plane(x, masks) - (beside_a[...] + beside_b[...]))


def two_steps(near, far, center, edge_potential, potential, masks, first, edge, second):
    def row(q, carry):
        own, other = center[0, q], center[1, q]
        edge_near, edge_far = near[4 + q], far[q]
        first[0, q] = local(own, edge_near + other, potential[0], masks)
        first[1, q] = local(other, own + edge_far, potential[1], masks)
        edge[0, q] = local(edge_near, near[q] + own, edge_potential[0], masks)
        edge[1, q] = local(edge_far, other + far[4 + q], edge_potential[1], masks)
        second[0, q] = local(first[0, q], edge[0, q] + first[1, q], potential[0], masks)
        second[1, q] = local(first[1, q], first[0, q] + edge[1, q], potential[1], masks)
        return carry

    lax.fori_loop(0, 4, row, 0)


def spread(parts, lanes):
    total = jnp.concatenate([rows8(parts[k : k + 8]) for k in range(0, len(parts), 8)], 0)
    summed = jnp.sum(total, axis=1, keepdims=True)
    lane = lax.broadcasted_iota(jnp.int32, total.shape, 1)
    return jnp.where(lane == lanes, summed, 0.0)


def moments_kernel(slopes, *refs):
    near, far, center, edge_potential, potential, masks, basis_own, basis_other = refs[:8]
    refs = refs[8:]
    if slopes:
        wave_x, wave_y, wave_z = refs[:3]
        refs = refs[3:]
    first, second, out, edge = refs
    two_steps(near, far, center, edge_potential, potential, masks, first, edge, second)
    count = 32 if slopes else 16

    def projector(j, total):
        atom = j // PRJ_ATOM
        parts = [[None] * 4 for _ in range(7)]
        for plane, basis in ((0, basis_own), (1, basis_other)):
            beta = basis[j, 0]
            wide = basis[j, 1] + potential[plane] * beta
            if slopes:
                beta_y, beta_z = beta * wave_y[atom], beta * wave_z[atom]
            for q in range(4):
                x = center[plane, q]
                found = [fold(x * beta), fold(x * wide)]
                found += [fold(first[plane, q] * wide), fold(second[plane, q] * wide)]
                if slopes:
                    found += [found[0] * wave_x[plane, atom]]
                    found += [fold(x * beta_y), fold(x * beta_z)]
                for k, value in enumerate(found):
                    parts[k][q] = value if plane == 0 else parts[k][q] + value
        flat = [parts[k][q] for k in range(7 if slopes else 4) for q in range(4)]
        flat += [jnp.zeros((8, LANES), f32)] * (count - len(flat))
        return total + spread(flat, j)

    out[...] = lax.fori_loop(0, PRJ, projector, jnp.zeros((count, LANES), f32))


def gram_kernel(basis, potentials, out, wide):
    for k in range(2):
        for j in range(PRJ):
            wide[k, j] = basis[j, 1] + potentials[k] * basis[j, 0]

    def projector(j, total):
        beta, wide_a, wide_b = basis[j, 0], wide[0, j], wide[1, j]
        for group in range(2):
            members = range(8 * group, 8 * group + 8)
            found = [
                [fold(beta * basis[i, 0]) for i in members],
                [fold(wide_a * basis[i, 0]) for i in members],
                [fold(wide_a * wide[0, i]) for i in members],
                [fold(wide_b * basis[i, 0]) for i in members],
                [fold(wide_b * wide[1, i]) for i in members],
            ]
            for k, parts in enumerate(found):
                total[group] = total[group] + spread(parts, PRJ * (k + 1) + j)
        return total

    start = [jnp.zeros((8, LANES), f32)] * 2
    total = lax.fori_loop(0, PRJ, projector, start)
    out[...] = jnp.concatenate(total, 0)


def times_i(x):
    row = lax.broadcasted_iota(jnp.int32, (8, LANES), 0)
    return jnp.where(row < 2, -pltpu.roll(x, 6, 0), pltpu.roll(x, 2, 0))


def coefficients_kernel(later, flags, received, strengths, *refs):
    if later:
        gram, table = refs
    else:
        table, gram = refs
    upper, sign = flags[0], flags[1]
    sums = []
    for core in range(2):
        acc = received[core]
        for k in range(core + 2, 16, 2):
            acc = acc + received[k]
        sums.append(acc)
    if later:
        grams = gram[...]
    else:
        grams = (sums[0] + sums[1])[:PRJ]
        gram[...] = grams
    mine = jnp.where(upper > 0.5, sums[1], sums[0])[:PRJ]
    lane = lax.broadcasted_iota(jnp.int32, (PRJ, LANES), 1)
    valid = lane < PRJ

    def block(k):
        return jnp.where(valid, pltpu.roll(grams, LANES - PRJ * (k + 1), 1), 0.0)

    use_second = (upper < 0.5) if later else (upper > 0.5)
    g0 = block(0)
    g1 = jnp.where(use_second, block(3), block(1))
    g2 = jnp.where(use_second, block(4), block(2))
    weight = strengths[...]

    def moment(k):
        rolled = mine if k == 0 else pltpu.roll(mine, PRJ - 4 * k, 0)
        return jnp.where(valid, rolled, 0.0)[:8]

    def apply(c, g):
        return jnp.dot(c[:, :PRJ], g, precision=highest, preferred_element_type=f32)

    c0 = weight * moment(0)
    c1 = weight * (moment(1) + apply(c0, g0))
    c2 = weight * (moment(2) + apply(c0, g1) + apply(c1, g0))
    c3 = weight * (moment(3) + apply(c0, g2) + apply(c1, g1) + apply(c2, g0))
    e0 = times_i((sign * half_step) * c0 + (sign * A3) * c2) + A2 * c1 + A4 * c3
    e1 = A2 * c0 + A4 * c2
    row = lax.broadcasted_iota(jnp.int32, (PRJ, LANES), 0)
    for k, c in enumerate((c0, c1, e0, e1)):
        for q in range(4):
            wide = jnp.broadcast_to(c[q : q + 1], (PRJ, LANES))
            column = jnp.sum(jnp.where(row == lane, wide, 0.0), axis=1, keepdims=True)
            for j in range(PRJ):
                table[j, k, q] = jnp.broadcast_to(column[j : j + 1], (8, LANES))


def middle_kernel(flags, center, first, second, basis_own, basis_other, potential, table, u2, partial):
    sign = flags[1]

    def tile(i, carry):
        rows = pl.ds(pl.multiple_of(i * 8, 8), 8)
        for plane, basis in ((0, basis_own), (1, basis_other)):
            v = potential[plane, rows]
            ahead = [second[plane, q, rows] for q in range(4)]
            moved = [first[plane, q, rows] for q in range(4)]
            mixed = [-moved[2], -moved[3], moved[0], moved[1]]
            result = [
                center[plane, q, rows] + (sign * half_step) * mixed[q] + A2 * ahead[q]
                for q in range(4)
            ]
            for j in range(PRJ):
                beta = basis[j, 0, rows]
                wide = basis[j, 1, rows] + v * beta
                for q in range(4):
                    ahead[q] = ahead[q] + table[j, 0, q] * wide + table[j, 1, q] * beta
                    result[q] = result[q] + table[j, 3, q] * wide + table[j, 2, q] * beta
            for q in range(4):
                u2[plane, q, rows] = ahead[q]
                partial[plane, q, rows] = result[q]
        return carry

    lax.fori_loop(0, ROWS // 8, tile, 0)


def last_kernel(flags, near, far, center, edge_potential, potential, masks, partial, out, first, edge, second):
    two_steps(near, far, center, edge_potential, potential, masks, first, edge, second)
    sign = flags[1]
    for plane in range(2):
        for q in range(4):
            mixed = -first[plane, q + 2] if q < 2 else first[plane, q - 2]
            out[plane, q] = partial[plane, q] + (sign * A3) * mixed + A4 * second[plane, q]


def swap_core(x):
    return lax.ppermute(x, "space", [(i, i ^ 1) for i in range(16)])


def body(
    psi_start,
    adjoint_end,
    potential_now,
    potential_next,
    projector_tiles,
    tile_map,
    strengths,
    positions,
):
    space, band = lax.axis_index("space"), lax.axis_index("band")
    lower = (space % 2) == 0
    masks = jnp.asarray(neighbour_masks())
    plane_shape = (ROWS, LANES)
    psi = psi_start.reshape((4,) + plane_shape)
    adjoint = adjoint_end.reshape((4,) + plane_shape)
    potentials = jnp.stack([potential_now, potential_next]).reshape((2,) + plane_shape)
    reach = lax.dynamic_index_in_dim(tile_map.reshape(-1, ROWS), band // PRJ_ATOM, 0, False)
    beta = projector_tiles.reshape(plane_shape) * reach.astype(f32)[:, None]
    flags = jnp.stack([jnp.where(lower, 0.0, 1.0), jnp.where(lower, -1.0, 1.0)]).astype(f32)

    kept = jnp.where(lower, psi, adjoint)
    given = jnp.where(lower, adjoint, psi)
    beta_near = lax.ppermute(
        beta, "space", [(i, (i + 1) % 16 if i % 2 else (i - 1) % 16) for i in range(16)]
    )
    other = swap_core(jnp.concatenate([given, potentials, beta[None]], 0))
    center = jnp.stack([kept, other[:4]])
    potentials_other = other[4:6]

    from_near = [(i, (i + 2) % 16 if i % 2 == 0 else (i - 2) % 16) for i in range(16)]
    from_far = [(j, i) for i, j in from_near]

    def exchange(fields, near_extra=None, far_extra=None):
        flat = fields.reshape((8,) + plane_shape)
        near = flat if near_extra is None else jnp.concatenate([flat, near_extra], 0)
        far = flat if far_extra is None else jnp.concatenate([flat, far_extra], 0)
        return (lax.ppermute(near, "space", from_near), lax.ppermute(far, "space", from_far))

    near, far = exchange(center, potentials_other, potentials)

    own_pair = call(projector_kernel, (2,) + plane_shape, [beta, other[6], beta_near, masks])
    basis_own = lax.all_to_all(
        jnp.broadcast_to(own_pair[None], (PRJ, 2) + plane_shape), "band", 0, 0, tiled=True
    )
    basis_other = swap_core(basis_own)

    now_own, next_own = (potentials[0], potentials[1])
    own_a, own_b = jnp.where(lower, now_own, next_own), jnp.where(lower, next_own, now_own)
    far_side, near_side = far[8:10], near[8:10]
    stacked = jnp.stack([potentials, potentials_other, near_side, far_side], 1)
    early = jnp.where(lower, stacked[0], stacked[1])
    late = jnp.where(lower, stacked[1], stacked[0])

    plane = space + jnp.stack([jnp.int32(0), 1 - 2 * (space % 2)])
    flat = jnp.arange(ROWS * LANES, dtype=jnp.int32)
    wave_x = jnp.sin(
        2.0 * math.pi / 16 * (plane[:, None] - positions[0][None, :]).astype(f32)
    )
    wave_x = jnp.broadcast_to(wave_x[:, :, None, None], (2, 4, 8, LANES))
    wave_y = jnp.sin(
        2.0 * math.pi / NY * (flat[None, :] // NZ - positions[1][:, None]).astype(f32)
    ).reshape((4,) + plane_shape)
    wave_z = jnp.sin(
        2.0 * math.pi / NZ * (flat[None, :] % NZ - positions[2][:, None]).astype(f32)
    ).reshape((4,) + plane_shape)

    gram_part = call(
        gram_kernel,
        (PRJ, LANES),
        [basis_own, potentials],
        scratch=[pltpu.VMEM((2, PRJ) + plane_shape, f32)],
    )
    weight = jnp.pad(strengths, (0, LANES - PRJ)).reshape(1, LANES)
    fields_shape = (2, 4) + plane_shape
    field_scratch = pltpu.VMEM(fields_shape, f32)

    def total(part):
        return lax.all_to_all(
            jnp.broadcast_to(part[None], (16,) + part.shape), "space", 0, 0, tiled=True
        )

    def half(center, near, far, around, gram, slopes):
        v, edge_v = around[:2], around[2:]
        first, second, part = call(
            functools.partial(moments_kernel, slopes is not None),
            [fields_shape, fields_shape, (16 if slopes is None else 32, LANES)],
            [near, far, center, edge_v, v, masks, basis_own, basis_other] + list(slopes or ()),
            scratch=[field_scratch],
        )
        table_shape = (PRJ, 4, 4, 8, LANES)
        if gram is None:
            received = total(part + gram_part)
            table, gram = call(
                functools.partial(coefficients_kernel, False),
                [table_shape, (PRJ, LANES)],
                [flags, received, weight],
                scalars=1,
            )
        else:
            received = total(part)
            table = call(
                functools.partial(coefficients_kernel, True),
                table_shape,
                [flags, received, weight, gram],
                scalars=1,
            )
        u2, partial = call(
            middle_kernel,
            [fields_shape, fields_shape],
            [flags, center, first, second, basis_own, basis_other, v, table],
            scalars=1,
        )
        near, far = exchange(u2)
        result = call(
            last_kernel,
            fields_shape,
            [flags, near, far, u2, edge_v, v, masks, partial],
            scratch=[field_scratch] * 3,
            scalars=1,
        )
        return result, received, gram

    mid, _, gram = half(center, near, far, early, None, None)
    near, far = exchange(mid)
    mine, yours = mid[0], swap_core(mid[1])
    turned = mine[:2] * yours[2:] - mine[2:] * yours[:2]
    density = (-2.0 * half_step * flags[1]) * jnp.sum(turned, axis=0)
    end, received, _ = half(mid, near, far, late, gram, (wave_x, wave_y, wave_z))

    sums = jnp.sum(received.reshape(8, 2, 32, LANES), axis=0)[:, :, :PRJ]
    value, slope = sums[:, :4], sums[:, 16:28].reshape(2, 3, 4, PRJ)
    products = value[:1] * slope[1:] + value[1:] * slope[:1]
    weighted = jnp.sum(products[0], axis=1) * strengths
    forces = jnp.sum(weighted.reshape(3, 4, PRJ_ATOM), axis=2).reshape(12)
    parts = jnp.concatenate(
        [density.reshape(16, 576), jnp.broadcast_to(forces[None], (16, 12))], axis=1
    )
    parts = jnp.pad(parts, ((0, 0), (0, 1024 - 588))).reshape(16, 8, LANES)
    shared = jnp.sum(lax.all_to_all(parts, "band", 0, 0, tiled=True), axis=0).reshape(1024)

    swapped = swap_core(end[1])
    psi_end = jnp.where(lower, end[0], swapped).reshape(psi_start.shape)
    adjoint_start = jnp.where(lower, swapped, end[0]).reshape(adjoint_end.shape)
    return (
        psi_end,
        adjoint_start,
        shared[:576].reshape(1, 576),
        shared[576:588].reshape(3, 4) / NB,
    )


def solution(mesh):
    return jax.shard_map(
        body,
        mesh=mesh,
        in_specs=(
            P(None, "band", "space", None),
            P(None, "band", "space", None),
            P("space", None),
            P("space", None),
            P("band", "space", None),
            P(None, "space", None),
            P(),
            P(),
        ),
        out_specs=(
            P(None, "band", "space", None),
            P(None, "band", "space", None),
            P("space", "band"),
            P(),
        ),
        check_vma=False,
    )
```

```python
import functools
import math

import jax
import jax.numpy as jnp
import numpy as np
from jax import lax
from jax.experimental import pallas as pl
from jax.experimental.pallas import tpu as pltpu
from jax.sharding import PartitionSpec as P

NB = 32
NY = 96
NZ = 96
ROWS = 72
LANES = 128
PRJ = 16
PRJ_ATOM = 4

half_step = 0.025
kinetic_scale = 3.125
highest = lax.Precision.HIGHEST
f32 = jnp.float32

A2 = -(half_step**2) / 2.0
A3 = -(half_step**3) / 6.0
A4 = half_step**4 / 24.0


def columns():
    return (np.arange(ROWS * LANES, dtype=np.int32) % NZ).reshape(ROWS, LANES)


TILES = [slice(8 * t, 8 * t + 8) for t in range(ROWS // 8)]


def next_rows(ref, index, t, x, sub):
    if t < len(TILES) - 1:
        return ref[index + (slice(8 * t + 1, 8 * t + 9),)]
    wrapped = jnp.broadcast_to(ref[index + (slice(0, 1),)], (8, LANES))
    return jnp.where(sub == 7, wrapped, pltpu.roll(x, 7, 0))


def previous_rows(ref, index, t, x, sub):
    if t > 0:
        return ref[index + (slice(8 * t - 1, 8 * t + 7),)]
    wrapped = jnp.broadcast_to(ref[index + (slice(ROWS - 1, ROWS),)], (8, LANES))
    return jnp.where(sub == 0, wrapped, pltpu.roll(x, 1, 0))


def kinetic_plane(ref, index, column, beside, store, scratch):
    lane = lax.broadcasted_iota(jnp.int32, (8, LANES), 1)
    sub = lax.broadcasted_iota(jnp.int32, (8, LANES), 0)
    for t, rows in enumerate(TILES):
        x = ref[index + (rows,)]
        after, before = next_rows(ref, index, t, x, sub), previous_rows(ref, index, t, x, sub)
        up = pltpu.roll(jnp.where(lane >= 96, x, after), 32, 1)
        down = pltpu.roll(jnp.where(lane < 32, x, before), 96, 1)
        place = column[rows]
        scratch[0, rows] = up + down
        scratch[1, rows] = jnp.where(place == 0, down, x)
        scratch[2, rows] = jnp.where(place == NZ - 1, up, x)
    for t, rows in enumerate(TILES):
        ahead, behind = scratch[1, rows], scratch[2, rows]
        after = next_rows(scratch, (1,), t, ahead, sub)
        before = previous_rows(scratch, (2,), t, behind, sub)
        up = pltpu.roll(jnp.where(lane >= 1, ahead, after), 127, 1)
        down = pltpu.roll(jnp.where(lane < 127, behind, before), 1, 1)
        around = scratch[0, rows] + (up + down)
        x = ref[index + (rows,)]
        store(rows, x, kinetic_scale * (6.0 * x - around - beside(rows)))


def fold(x):
    return jnp.sum(x.reshape(ROWS // 8, 8, LANES), axis=0)


def rows8(parts):
    sub = lax.broadcasted_iota(jnp.int32, (8, LANES), 0)
    low = sub < 4
    parts = [
        jnp.where(low, a, b) + pltpu.roll(jnp.where(low, b, a), 4, 0)
        for a, b in zip(parts[:4], parts[4:])
    ]
    for step in (2, 1):
        first = (sub & step) == 0
        parts = [
            jnp.where(first, a + pltpu.roll(a, 8 - step, 0), b + pltpu.roll(b, step, 0))
            for a, b in zip(parts[:step], parts[step:])
        ]
    return parts[0]


def params(mib):
    return pltpu.CompilerParams(vmem_limit_bytes=mib * 2**20)


VMEM = pl.BlockSpec(memory_space=pltpu.VMEM)
SMEM = pl.BlockSpec(memory_space=pltpu.SMEM)


def call(kernel, outs, args, scratch=(), scalars=0, mib=8, cost=None):
    specs = [SMEM] * scalars + [VMEM] * (len(args) - scalars)
    single = not isinstance(outs, list)
    shapes = [
        o if hasattr(o, "dtype") else jax.ShapeDtypeStruct(o, f32)
        for o in ([outs] if single else outs)
    ]
    result = pl.pallas_call(
        kernel,
        out_shape=shapes,
        in_specs=specs,
        out_specs=[VMEM] * len(shapes),
        scratch_shapes=list(scratch),
        compiler_params=params(mib),
        cost_estimate=cost,
    )(*args)
    return result[0] if single else result


def mask_kernel(atom, values, tile_map, out):
    reach = tile_map[pl.ds(atom[0], 1)].astype(f32)
    row = lax.broadcasted_iota(jnp.int32, (ROWS, ROWS), 0)
    lane = lax.broadcasted_iota(jnp.int32, (ROWS, ROWS), 1)
    wide = jnp.where(row == lane, jnp.broadcast_to(reach, (ROWS, ROWS)), 0.0)
    share(out, values[...] * jnp.sum(wide, axis=1, keepdims=True))


def give_kernel(flags, psi, adjoint, now, later, kept, message, own):
    lower = flags[0] < 0.5
    for q in range(4):
        a, b = psi[q], adjoint[q]
        kept[q] = jnp.where(lower, a, b)
        message[q] = jnp.where(lower, b, a)
    own[0] = now[...]
    own[1] = later[...]
    message[4] = now[...]
    message[5] = later[...]


def pack_kernel(kept, own, other, near, far, center):
    center[0] = kept[...]
    center[1] = other[0:4]
    near[0:4] = kept[...]
    near[4:10] = other[...]
    far[0:4] = kept[...]
    far[4:8] = other[0:4]
    far[8:10] = own[...]


def kinetic_kernel(basis, basis_other, basis_near, column, out, work):
    def projector(pair, carry):
        for k in range(2):
            j = 2 * pair + k

            def store(rows, x, kinetic):
                out[j, rows] = kinetic

            def beside(rows):
                return basis_other[j, rows] + basis_near[j, rows]

            kinetic_plane(basis, (j,), column, beside, store, work.at[k])
        return carry

    lax.fori_loop(0, PRJ // 2, projector, 0)


def two_steps(near, far, center, potential, column, first, edge, second, work):
    def local(source, index, beside, v, out, place, k):
        def store(rows, x, kinetic):
            out[place + (rows,)] = kinetic + v[rows] * x

        kinetic_plane(source, index, column, beside, store, work.at[k])

    def row(q, carry):
        own, other = (0, q), (1, q)
        local(
            center, own, lambda r: near[4 + q, r] + center[1, q, r], potential.at[0], first, own, 0
        )
        local(center, other, lambda r: center[0, q, r] + far[q, r], potential.at[1], first, other, 1)
        local(
            near, (4 + q,), lambda r: near[q, r] + center[0, q, r], potential.at[2], edge, own, 2
        )
        local(
            far, (q,), lambda r: center[1, q, r] + far[4 + q, r], potential.at[3], edge, other, 3
        )
        local(first, own, lambda r: edge[0, q, r] + first[1, q, r], potential.at[0], second, own, 0)
        local(
            first, other, lambda r: first[0, q, r] + edge[1, q, r], potential.at[1], second, other, 1
        )
        return carry

    lax.fori_loop(0, 4, row, 0)


def spread(parts, lanes):
    total = jnp.concatenate([rows8(parts[k : k + 8]) for k in range(0, len(parts), 8)], 0)
    summed = jnp.sum(total, axis=1, keepdims=True)
    lane = lax.broadcasted_iota(jnp.int32, total.shape, 1)
    return jnp.where(lane == lanes, summed, 0.0)


def start_kernel(flags, near, far, center, own, other, column, first, second, early, late, edge, work):
    lower = flags[0] < 0.5
    pairs = [(own.at[0], own.at[1]), (other.at[4], other.at[5])]
    pairs += [(near.at[8], near.at[9]), (far.at[8], far.at[9])]
    for k, (a, b) in enumerate(pairs):
        a, b = a[...], b[...]
        early[k] = jnp.where(lower, a, b)
        late[k] = jnp.where(lower, b, a)
    two_steps(near, far, center, early, column, first, edge, second, work)


def project(basis, potential, kinds, count):
    def projector(j, total):
        parts = [[None] * 4 for _ in kinds]
        for plane in range(2):
            beta = basis[plane][j]
            wide = None if len(basis) == 2 else basis[2 + plane][j] + potential[plane] * beta
            for k, (field, by) in enumerate(kinds):
                factor = wide if by == "wide" else beta if by is None else by(plane, j, beta)
                for q in range(4):
                    value = fold(field[plane, q] * factor)
                    parts[k][q] = value if plane == 0 else parts[k][q] + value
        flat = [value for part in parts for value in part]
        flat += [jnp.zeros((8, LANES), f32)] * (count - len(flat))
        return total + spread(flat, j)

    return lax.fori_loop(0, PRJ, projector, jnp.zeros((count, LANES), f32))


def share(out, value):
    def copy(k, carry):
        out[k] = value
        return carry

    lax.fori_loop(0, 16, copy, 0)


def split(x):
    high = x.astype(jnp.bfloat16)
    return high, (x - high.astype(f32)).astype(jnp.bfloat16)


def put(target, row, lanes, value, offset):
    high, low = split(value)
    target[row : row + PRJ, lanes] = high
    target[row + offset : row + offset + PRJ, lanes] = low


def flat_rows(ref, s, count):
    return ref[pl.ds(s, count, stride=ROWS)]


def lanes_at(s):
    return pl.ds(pl.multiple_of(s * LANES, LANES), LANES)


def products(a, b):
    return lax.dot_general(a[...], b[...], (((1,), (1,)), ((), ())), preferred_element_type=f32)


def gram_kernel(basis, kinetic, early, late, out, flat):
    def row(s, carry):
        beta, moved = flat_rows(basis, s, PRJ), flat_rows(kinetic, s, PRJ)
        at = lanes_at(s)
        put(flat, 0, at, beta, 64)
        for k, v in enumerate((early, late)):
            put(flat, PRJ * (k + 1), at, moved + v[0, pl.ds(s, 1)] * beta, 64)
        return carry

    for k in (48, 112):
        flat[k : k + PRJ] = jnp.zeros((PRJ, ROWS * LANES), jnp.bfloat16)
    lax.fori_loop(0, ROWS, row, 0, unroll=8)
    both = products(flat, flat)
    both = both[:64] + both[64:]
    both = both + pltpu.roll(both, 64, 1)
    lane = lax.broadcasted_iota(jnp.int32, (PRJ, LANES), 1)
    out[...] = (
        jnp.where((lane >= 16) & (lane < 64), pltpu.roll(both[:16], 16, 1), 0.0)
        + jnp.where((lane >= 64) & (lane < 80), pltpu.roll(both[16:32], 48, 1), 0.0)
        + jnp.where((lane >= 80) & (lane < 96), pltpu.roll(both[32:48], 48, 1), 0.0)
    )


def put_fields(fields, flat):
    def row(s, carry):
        at = lanes_at(s)
        values = [flat_rows(field, s, 8) for field in fields]
        for k in range(0, len(values), 2):
            pair = values[k : k + 2]
            pair = pair if len(pair) == 2 else pair * 2
            put(flat, 8 * k, at, jnp.concatenate(pair, 0), 32)
        return carry

    lax.fori_loop(0, ROWS, row, 0, unroll=8)


def put_basis(own, other, own_k, other_k, potential, flat):
    def row(s, carry):
        at = lanes_at(s)
        for plane, (b, k) in enumerate(((own, own_k), (other, other_k))):
            beta, moved = flat_rows(b, s, PRJ), flat_rows(k, s, PRJ)
            put(flat, 2 * PRJ * plane, at, beta, 64)
            put(flat, 2 * PRJ * plane + PRJ, at, moved + potential[plane, pl.ds(s, 1)] * beta, 64)
        return carry

    lax.fori_loop(0, ROWS, row, 0, unroll=8)


def field_moments(fields_flat, basis_flat, count):
    both = products(fields_flat, basis_flat)
    both = both[:32] + both[32:]
    both = both + pltpu.roll(both, 64, 1)
    result = []
    for k in range(count):
        part = both[8 * k : 8 * k + 8]
        result.append(part + pltpu.roll(pltpu.roll(part, 96, 1), 4, 0))
    return result


def stack_rows(a, b):
    sub = lax.broadcasted_iota(jnp.int32, (8, LANES), 0)
    lane = lax.broadcasted_iota(jnp.int32, (8, LANES), 1)
    return jnp.where(lane < PRJ, jnp.where(sub < 4, a, pltpu.roll(b, 4, 0)), 0.0)


def early_moments_kernel(center, first, second, own, other, out, ahead_flat, fields_flat, basis_flat):
    put_fields((center, first, second), fields_flat)

    def row(s, carry):
        at = lanes_at(s)
        for plane, b in enumerate((own, other)):
            put(basis_flat, 2 * PRJ * plane, at, flat_rows(b, s, PRJ), 64)
        return carry

    for k in (16, 48, 80, 112):
        basis_flat[k : k + PRJ] = jnp.zeros((PRJ, ROWS * LANES), jnp.bfloat16)
    lax.fori_loop(0, ROWS, row, 0, unroll=8)
    found = field_moments(fields_flat, basis_flat, 3)
    out[...] = jnp.concatenate([stack_rows(found[0], found[1]), stack_rows(found[2], 0.0 * found[2])], 0)
    ahead_flat[0:16] = fields_flat[16:32]
    ahead_flat[16:32] = fields_flat[48:64]


def moments_kernel(known, ahead_flat, own, other, own_k, other_k, potential, gram, out, basis_flat):
    def row(s, carry):
        at = lanes_at(s)
        for plane, (b, k) in enumerate(((own, own_k), (other, other_k))):
            wide = flat_rows(k, s, PRJ) + potential[plane, pl.ds(s, 1)] * flat_rows(b, s, PRJ)
            put(basis_flat, PRJ * plane, at, wide, 32)
        return carry

    lax.fori_loop(0, ROWS, row, 0, unroll=8)
    both = products(ahead_flat, basis_flat)
    both = both[:8] + both[16:24]
    both = both[:, :32] + both[:, 32:]
    both = jnp.concatenate([both, jnp.zeros((8, LANES - 32), f32)], 1)
    wide = both + pltpu.roll(pltpu.roll(both, LANES - PRJ, 1), 4, 0)
    moments = jnp.concatenate([known[...][:8], known[...][8:] + stack_rows(0.0 * wide, wide)], 0)
    share(out, moments + gram[...])


def middle_moments_kernel(
    center, potential, own, other, own_k, other_k, wave_x, wave_y, wave_z, out, basis_flat
):
    kinds = [
        (center, None),
        (center, "wide"),
        (center, lambda plane, j, beta: beta * wave_x[plane, j // PRJ_ATOM, 0:1]),
        (center, lambda plane, j, beta: beta * wave_y[j // PRJ_ATOM]),
        (center, lambda plane, j, beta: beta * wave_z[j // PRJ_ATOM]),
    ]
    out[...] = project((own, other, own_k, other_k), potential, kinds, 24)
    flat = [x.reshape(PRJ * ROWS, LANES) for x in (own, other, own_k, other_k)]
    put_basis(*flat, potential, basis_flat)


def second_kernel(
    near, far, center, potential, column, basis_flat, known, first, second, out, edge, work, fields_flat
):
    two_steps(near, far, center, potential, column, first, edge, second, work)
    put_fields([x.reshape(8 * ROWS, LANES) for x in (first, second)], fields_flat)
    found = [pltpu.roll(x, LANES - PRJ, 1) for x in field_moments(fields_flat, basis_flat, 2)]
    value = known[...]
    share(out, jnp.concatenate([value[:8], stack_rows(*found), value[8:]], 0))


def times_i(x):
    row = lax.broadcasted_iota(jnp.int32, (8, LANES), 0)
    return jnp.where(row < 2, -pltpu.roll(x, 6, 0), pltpu.roll(x, 2, 0))


def coefficients(later, flags, received, strengths, gram):
    upper, sign = flags[0], flags[1]
    sums = []
    for core in range(2):
        acc = received[core]
        for k in range(core + 2, 16, 2):
            acc = acc + received[k]
        sums.append(acc)
    mine = jnp.where(upper > 0.5, sums[1], sums[0])[:PRJ]
    lane = lax.broadcasted_iota(jnp.int32, (PRJ, LANES), 1)
    valid = lane < PRJ
    if later:
        grams = gram[...]
    else:
        theirs = jnp.where(upper > 0.5, sums[0], sums[1])[:PRJ]
        turned = jnp.where(
            (lane >= 48) & (lane < 64) | (lane >= 80),
            pltpu.roll(theirs, PRJ, 1),
            pltpu.roll(theirs, LANES - PRJ, 1),
        )
        grams = mine + jnp.where(lane < 32, theirs, turned)
        gram[...] = grams

    def block(k):
        return jnp.where(valid, pltpu.roll(grams, LANES - PRJ * (k + 1), 1), 0.0)

    g0 = block(0)
    g1, g2 = (block(2), block(4)) if later else (block(1), block(3))
    weight = strengths[...]

    def moment(k):
        rolled = mine if k == 0 else pltpu.roll(mine, PRJ - 4 * k, 0)
        return jnp.where(valid, rolled, 0.0)[:8]

    def apply(c, g):
        return jnp.dot(c[:, :PRJ], g, precision=highest, preferred_element_type=f32)

    c0 = weight * moment(0)
    c1 = weight * (moment(1) + apply(c0, g0))
    c2 = weight * (moment(2) + apply(c0, g1) + apply(c1, g0))
    c3 = weight * (moment(3) + apply(c0, g2) + apply(c1, g1) + apply(c2, g0))
    e0 = times_i((sign * half_step) * c0 + (sign * A3) * c2) + A2 * c1 + A4 * c3
    e1 = A2 * c0 + A4 * c2
    return c0, c1, e0, e1


def spread_table(table, sets):
    row = lax.broadcasted_iota(jnp.int32, (PRJ, LANES), 0)
    lane = lax.broadcasted_iota(jnp.int32, (PRJ, LANES), 1)
    for k, c in enumerate(sets):
        for q in range(4):
            wide = jnp.broadcast_to(c[q : q + 1], (PRJ, LANES))
            column = jnp.sum(jnp.where(row == lane, wide, 0.0), axis=1, keepdims=True)
            for j in range(PRJ):
                table[j, k, q] = jnp.broadcast_to(column[j : j + 1], (8, LANES))


def combine(out, start, basis, potential, table):
    def tile(i, carry):
        rows = pl.ds(pl.multiple_of(i * 8, 8), 8)
        for plane in range(2):
            v = potential[plane, rows]
            total = start(plane, rows)
            for j in range(PRJ):
                beta = basis[plane][j, rows]
                wide = basis[2 + plane][j, rows] + v * beta
                for q in range(4):
                    total[q] = total[q] + table[j, 0, q] * wide + table[j, 1, q] * beta
            for q in range(4):
                out[plane, q, rows] = total[q]
        return carry

    lax.fori_loop(0, ROWS // 8, tile, 0)


def advance_kernel(later, flags, received, strengths, second, own, other, own_k, other_k, potential, *refs):
    if later:
        gram, out, rest, table = refs
    else:
        out, rest, gram, table = refs
    c0, c1, e0, e1 = coefficients(later, flags, received, strengths, gram)
    rest[0] = e1
    rest[1] = e0
    spread_table(table, (c0, c1))

    def start(plane, rows):
        return [second[plane, q, rows] for q in range(4)]

    combine(out, start, (own, other, own_k, other_k), potential, table)


def partial_kernel(flags, center, first, second, own, other, own_k, other_k, potential, rest, out, table):
    sign = flags[1]
    spread_table(table, (rest[0], rest[1]))

    def start(plane, rows):
        moved = [first[plane, q, rows] for q in range(4)]
        mixed = [-moved[2], -moved[3], moved[0], moved[1]]
        return [
            center[plane, q, rows] + (sign * half_step) * mixed[q] + A2 * second[plane, q, rows]
            for q in range(4)
        ]

    combine(out, start, (own, other, own_k, other_k), potential, table)


def last_kernel(flags, near, far, center, potential, column, partial, out, first, edge, second, work):
    two_steps(near, far, center, potential, column, first, edge, second, work)
    sign = flags[1]
    for plane in range(2):
        for q in range(4):
            mixed = -first[plane, q + 2] if q < 2 else first[plane, q - 2]
            out[plane, q] = partial[plane, q] + (sign * A3) * mixed + A4 * second[plane, q]


def payload_kernel(flags, mine, yours, received, strengths, out):
    turned = [mine[0, q] * yours[q + 2] - mine[0, q + 2] * yours[q] for q in range(2)]
    density = (-2.0 * half_step * flags[1]) * (turned[0] + turned[1])
    sums = []
    for core in range(2):
        acc = received[core]
        for k in range(core + 2, 16, 2):
            acc = acc + received[k]
        sums.append(acc)
    forces = []
    for q in range(3):
        rows = slice(16 + 4 * q, 20 + 4 * q)
        products = sums[0][:4] * sums[1][rows] + sums[1][:4] * sums[0][rows]
        forces.append(strengths[...] * jnp.sum(products, axis=0, keepdims=True))
    for k in range(16):
        first = 9 * k // 2
        out[k] = jnp.concatenate([density[first : first + 5]] + forces, 0)


def outcome_kernel(odd, received, density, forces):
    total = received[0]
    for k in range(1, 16):
        total = total + received[k]
    lane = lax.broadcasted_iota(jnp.int32, (1, LANES), 1)
    moved = pltpu.roll(total, 64, 1)
    for k in range(5):
        start = total[k : k + 1]
        shifted = jnp.where(lane < 64, moved[k : k + 1], moved[min(k + 1, 4) : min(k + 1, 4) + 1])
        row = jnp.where(odd[0] > 0, shifted, start)
        width = min(LANES, 576 - k * LANES)
        density[:, k * LANES : k * LANES + width] = row[:, :width]
    atom = lax.broadcasted_iota(jnp.int32, (3, LANES), 1) // PRJ_ATOM
    column = lax.broadcasted_iota(jnp.int32, (3, 4), 1)
    result = jnp.zeros((3, 4), f32)
    for a in range(4):
        part = jnp.sum(jnp.where(atom == a, total[5:8], 0.0), axis=1, keepdims=True)
        result = jnp.where(column == a, part * (1.0 / NB), result)
    forces[...] = result


def swap_core(x):
    return lax.ppermute(x, "space", [(i, i ^ 1) for i in range(16)])


def fence(*values):
    return lax.optimization_barrier(values)


def body(
    psi_start,
    adjoint_end,
    potential_now,
    potential_next,
    projector_tiles,
    tile_map,
    strengths,
    positions,
):
    space, band = lax.axis_index("space"), lax.axis_index("band")
    lower = (space % 2) == 0
    column = jnp.asarray(columns())
    plane_shape = (ROWS, LANES)
    fields_shape = (2, 4) + plane_shape
    rows_shape = (PRJ,) + plane_shape
    flags = jnp.stack([jnp.where(lower, 0.0, 1.0), jnp.where(lower, -1.0, 1.0)]).astype(f32)
    atom = (band // PRJ_ATOM).astype(jnp.int32).reshape(1)
    odd = (band % 2).astype(jnp.int32).reshape(1)

    payload = call(
        mask_kernel,
        rows_shape,
        [atom, projector_tiles.reshape(plane_shape), tile_map.reshape(4, ROWS)],
        scalars=1,
    )
    basis_own = lax.all_to_all(payload, "band", 0, 0, tiled=True)

    kept, given, own = call(
        give_kernel,
        [(4,) + plane_shape, (6,) + plane_shape, (2,) + plane_shape],
        [
            flags,
            psi_start.reshape((4,) + plane_shape),
            adjoint_end.reshape((4,) + plane_shape),
            potential_now.reshape(plane_shape),
            potential_next.reshape(plane_shape),
        ],
        scalars=1,
    )
    other = swap_core(given)
    near_message, far_message, center = call(
        pack_kernel,
        [(10,) + plane_shape, (10,) + plane_shape, fields_shape],
        [kept, own, other],
    )

    from_near = [(i, (i + 2) % 16 if i % 2 == 0 else (i - 2) % 16) for i in range(16)]
    from_far = [(j, i) for i, j in from_near]
    beside = [(i, (i + 1) % 16 if i % 2 else (i - 1) % 16) for i in range(16)]

    def exchange(fields):
        flat = fields.reshape((8,) + plane_shape)
        return (lax.ppermute(flat, "space", from_near), lax.ppermute(flat, "space", from_far))

    near = lax.ppermute(near_message, "space", from_near)
    far = lax.ppermute(far_message, "space", from_far)

    basis_own, near, far, strengths, positions = fence(
        basis_own, near, far, strengths, positions
    )
    basis_near = lax.ppermute(basis_own, "space", beside)
    basis_other = swap_core(basis_own)

    field_scratch = pltpu.VMEM(fields_shape, f32)
    work_scratch = pltpu.VMEM((4, 3) + plane_shape, f32)
    first, second, early, late = call(
        start_kernel,
        [fields_shape, fields_shape, (4,) + plane_shape, (4,) + plane_shape],
        [flags, near, far, center, own, other, column],
        scratch=[field_scratch, work_scratch],
        scalars=1,
    )
    flat_shape = (PRJ * ROWS, LANES)
    fields_flat = (8 * ROWS, LANES)
    known, ahead_flat = call(
        early_moments_kernel,
        [(16, LANES), jax.ShapeDtypeStruct((32, ROWS * LANES), jnp.bfloat16)],
        [x.reshape(fields_flat) for x in (center, first, second)]
        + [x.reshape(flat_shape) for x in (basis_own, basis_other)],
        scratch=[
            pltpu.VMEM((64, ROWS * LANES), jnp.bfloat16),
            pltpu.VMEM((128, ROWS * LANES), jnp.bfloat16),
        ],
        mib=12,
    )
    basis_near, first, second, early, late, known = fence(
        basis_near, first, second, early, late, known
    )
    kinetic_own = call(
        kinetic_kernel,
        rows_shape,
        [basis_own, basis_other, basis_near, column],
        scratch=[work_scratch],
    )
    kinetic_other = swap_core(kinetic_own)
    gram_part = call(
        gram_kernel,
        (PRJ, LANES),
        [basis_own.reshape(flat_shape), kinetic_own.reshape(flat_shape), early, late],
        scratch=[pltpu.VMEM((128, ROWS * LANES), jnp.bfloat16)],
        mib=12,
    )
    kinetic_other, gram_part = fence(kinetic_other, gram_part)
    basis = [basis_own, basis_other, kinetic_own, kinetic_other]
    part = call(
        moments_kernel,
        (16, 16, LANES),
        [known, ahead_flat] + [x.reshape(flat_shape) for x in basis] + [early, gram_part],
        scratch=[pltpu.VMEM((64, ROWS * LANES), jnp.bfloat16)],
        mib=12,
    )

    table_scratch = pltpu.VMEM((PRJ, 2, 4, 8, LANES), f32)
    rest_shape = (2, 8, LANES)
    received = lax.all_to_all(part, "space", 0, 0, tiled=True)
    received, strengths, positions, space, first, second, early, late, center = fence(
        received, strengths, positions, space, first, second, early, late, center
    )
    plane = space + jnp.stack([jnp.int32(0), 1 - 2 * (space % 2)])
    flat = np.arange(ROWS * LANES, dtype=np.int32)
    wave_x = jnp.sin(
        2.0 * math.pi / 16 * (plane[:, None] - positions[0][None, :]).astype(f32)
    )
    wave_x = jnp.broadcast_to(wave_x[:, :, None, None], (2, 4, 8, LANES))
    wave_y = jnp.sin(
        2.0 * math.pi / NY * (jnp.asarray(flat // NZ)[None, :] - positions[1][:, None]).astype(f32)
    ).reshape((4,) + plane_shape)
    wave_z = jnp.sin(
        2.0 * math.pi / NZ * (jnp.asarray(flat % NZ)[None, :] - positions[2][:, None]).astype(f32)
    ).reshape((4,) + plane_shape)
    weight = jnp.pad(strengths, (0, LANES - PRJ)).reshape(1, LANES)
    u2, rest, gram = call(
        functools.partial(advance_kernel, False),
        [fields_shape, rest_shape, (PRJ, LANES)],
        [flags, received, weight, second] + basis + [early],
        scratch=[table_scratch],
        scalars=1,
    )

    def finish(center, first, second, around, u2, rest, parts=None):
        flat = u2.reshape((8,) + plane_shape)
        near = lax.ppermute(flat, "space", from_near)
        shared = None
        if parts is not None:
            flat, parts = fence(flat, parts)
            far = lax.ppermute(flat, "space", from_far)
            shared = lax.all_to_all(parts, "band", 0, 0, tiled=True)
            rest, shared = fence(rest, shared)
        partial = call(
            partial_kernel,
            fields_shape,
            [flags, center, first, second] + basis + [around, rest],
            scratch=[table_scratch],
            scalars=1,
        )
        if parts is None:
            flat, partial = fence(flat, partial)
            far = lax.ppermute(flat, "space", from_far)
        return shared, call(
            last_kernel,
            fields_shape,
            [flags, near, far, u2, around, column, partial],
            scratch=[field_scratch] * 3 + [work_scratch],
            scalars=1,
        )

    _, mid = finish(center, first, second, early, u2, rest)
    near, far = exchange(mid)
    yours = swap_core(mid[1])
    known, basis_flat = call(
        middle_moments_kernel,
        [(24, LANES), jax.ShapeDtypeStruct((128, ROWS * LANES), jnp.bfloat16)],
        [mid, late] + basis + [wave_x, wave_y, wave_z],
    )
    first, second, part = call(
        second_kernel,
        [fields_shape, fields_shape, (16, 32, LANES)],
        [near, far, mid, late, column, basis_flat, known],
        scratch=[
            field_scratch,
            work_scratch,
            pltpu.VMEM((64, ROWS * LANES), jnp.bfloat16),
        ],
    )
    part, yours = fence(part, yours)
    received = lax.all_to_all(part, "space", 0, 0, tiled=True)
    received, first, second, late, mid, yours = fence(received, first, second, late, mid, yours)
    u2, rest = call(
        functools.partial(advance_kernel, True),
        [fields_shape, rest_shape],
        [flags, received, weight, second] + basis + [late, gram],
        scratch=[table_scratch],
        scalars=1,
    )

    parts = call(
        payload_kernel, (16, 8, LANES), [flags, mid, yours, received, weight], scalars=1
    )
    shared, end = finish(mid, first, second, late, u2, rest, parts)
    density, forces = call(outcome_kernel, [(1, 576), (3, 4)], [odd, shared], scalars=1)

    swapped = swap_core(end[1])
    psi_end = jnp.where(lower, end[0], swapped).reshape(psi_start.shape)
    adjoint_start = jnp.where(lower, swapped, end[0]).reshape(adjoint_end.shape)
    return (psi_end, adjoint_start, density, forces)


def solution(mesh):
    return jax.shard_map(
        body,
        mesh=mesh,
        in_specs=(
            P(None, "band", "space", None),
            P(None, "band", "space", None),
            P("space", None),
            P("space", None),
            P("band", "space", None),
            P(None, "space", None),
            P(),
            P(),
        ),
        out_specs=(
            P(None, "band", "space", None),
            P(None, "band", "space", None),
            P("space", "band"),
            P(),
        ),
        check_vma=False,
    )
```

```python
import functools
import math

import jax
import jax.numpy as jnp
import numpy as np
from jax import lax
from jax.experimental import pallas as pl
from jax.experimental.pallas import tpu as pltpu
from jax.sharding import PartitionSpec as P

NB = 32
NY = 96
NZ = 96
ROWS = 72
LANES = 128
PRJ = 16
PRJ_ATOM = 4

half_step = 0.025
kinetic_scale = 3.125
highest = lax.Precision.HIGHEST
f32 = jnp.float32

A2 = -(half_step**2) / 2.0
A3 = -(half_step**3) / 6.0
A4 = half_step**4 / 24.0


def columns():
    return (np.arange(ROWS * LANES, dtype=np.int32) % NZ).reshape(ROWS, LANES)


TILES = [slice(8 * t, 8 * t + 8) for t in range(ROWS // 8)]


def next_rows(ref, index, t, x, sub):
    if t < len(TILES) - 1:
        return ref[index + (slice(8 * t + 1, 8 * t + 9),)]
    wrapped = jnp.broadcast_to(ref[index + (slice(0, 1),)], (8, LANES))
    return jnp.where(sub == 7, wrapped, pltpu.roll(x, 7, 0))


def previous_rows(ref, index, t, x, sub):
    if t > 0:
        return ref[index + (slice(8 * t - 1, 8 * t + 7),)]
    wrapped = jnp.broadcast_to(ref[index + (slice(ROWS - 1, ROWS),)], (8, LANES))
    return jnp.where(sub == 0, wrapped, pltpu.roll(x, 1, 0))


def kinetic_plane(ref, index, column, beside, store, scratch):
    lane = lax.broadcasted_iota(jnp.int32, (8, LANES), 1)
    sub = lax.broadcasted_iota(jnp.int32, (8, LANES), 0)
    for t, rows in enumerate(TILES):
        x = ref[index + (rows,)]
        after, before = next_rows(ref, index, t, x, sub), previous_rows(ref, index, t, x, sub)
        up = pltpu.roll(jnp.where(lane >= 96, x, after), 32, 1)
        down = pltpu.roll(jnp.where(lane < 32, x, before), 96, 1)
        place = column[rows]
        scratch[0, rows] = up + down
        scratch[1, rows] = jnp.where(place == 0, down, x)
        scratch[2, rows] = jnp.where(place == NZ - 1, up, x)
    for t, rows in enumerate(TILES):
        ahead, behind = scratch[1, rows], scratch[2, rows]
        after = next_rows(scratch, (1,), t, ahead, sub)
        before = previous_rows(scratch, (2,), t, behind, sub)
        up = pltpu.roll(jnp.where(lane >= 1, ahead, after), 127, 1)
        down = pltpu.roll(jnp.where(lane < 127, behind, before), 1, 1)
        around = scratch[0, rows] + (up + down)
        x = ref[index + (rows,)]
        store(rows, x, kinetic_scale * (6.0 * x - around - beside(rows)))


def fold(x):
    return jnp.sum(x.reshape(ROWS // 8, 8, LANES), axis=0)


def rows8(parts):
    sub = lax.broadcasted_iota(jnp.int32, (8, LANES), 0)
    low = sub < 4
    parts = [
        jnp.where(low, a, b) + pltpu.roll(jnp.where(low, b, a), 4, 0)
        for a, b in zip(parts[:4], parts[4:])
    ]
    for step in (2, 1):
        first = (sub & step) == 0
        parts = [
            jnp.where(first, a + pltpu.roll(a, 8 - step, 0), b + pltpu.roll(b, step, 0))
            for a, b in zip(parts[:step], parts[step:])
        ]
    return parts[0]


def params(mib):
    return pltpu.CompilerParams(vmem_limit_bytes=mib * 2**20)


VMEM = pl.BlockSpec(memory_space=pltpu.VMEM)
SMEM = pl.BlockSpec(memory_space=pltpu.SMEM)


def call(kernel, outs, args, scratch=(), scalars=0, mib=8, cost=None):
    specs = [SMEM] * scalars + [VMEM] * (len(args) - scalars)
    single = not isinstance(outs, list)
    shapes = [
        o if hasattr(o, "dtype") else jax.ShapeDtypeStruct(o, f32)
        for o in ([outs] if single else outs)
    ]
    result = pl.pallas_call(
        kernel,
        out_shape=shapes,
        in_specs=specs,
        out_specs=[VMEM] * len(shapes),
        scratch_shapes=list(scratch),
        compiler_params=params(mib),
        cost_estimate=cost,
    )(*args)
    return result[0] if single else result


def mask_kernel(atom, values, tile_map, out):
    reach = tile_map[pl.ds(atom[0], 1)].astype(f32)
    row = lax.broadcasted_iota(jnp.int32, (ROWS, ROWS), 0)
    lane = lax.broadcasted_iota(jnp.int32, (ROWS, ROWS), 1)
    wide = jnp.where(row == lane, jnp.broadcast_to(reach, (ROWS, ROWS)), 0.0)
    share(out, values[...] * jnp.sum(wide, axis=1, keepdims=True))


def give_kernel(flags, psi, adjoint, now, later, kept, message, own):
    lower = flags[0] < 0.5
    for q in range(4):
        a, b = psi[q], adjoint[q]
        kept[q] = jnp.where(lower, a, b)
        message[q] = jnp.where(lower, b, a)
    own[0] = now[...]
    own[1] = later[...]
    message[4] = now[...]
    message[5] = later[...]


def pack_kernel(kept, own, other, near, far, center):
    center[0] = kept[...]
    center[1] = other[0:4]
    near[0:4] = kept[...]
    near[4:10] = other[...]
    far[0:4] = kept[...]
    far[4:8] = other[0:4]
    far[8:10] = own[...]


def kinetic_kernel(basis, basis_other, basis_near, column, out, work):
    def projector(pair, carry):
        for k in range(2):
            j = 2 * pair + k

            def store(rows, x, kinetic):
                out[j, rows] = kinetic

            def beside(rows):
                return basis_other[j, rows] + basis_near[j, rows]

            kinetic_plane(basis, (j,), column, beside, store, work.at[k])
        return carry

    lax.fori_loop(0, PRJ // 2, projector, 0)


def two_steps(near, far, center, potential, column, first, edge, second, work):
    def local(source, index, beside, v, out, place, k):
        def store(rows, x, kinetic):
            out[place + (rows,)] = kinetic + v[rows] * x

        kinetic_plane(source, index, column, beside, store, work.at[k])

    def row(q, carry):
        own, other = (0, q), (1, q)
        local(
            center, own, lambda r: near[4 + q, r] + center[1, q, r], potential.at[0], first, own, 0
        )
        local(center, other, lambda r: center[0, q, r] + far[q, r], potential.at[1], first, other, 1)
        local(
            near, (4 + q,), lambda r: near[q, r] + center[0, q, r], potential.at[2], edge, own, 2
        )
        local(
            far, (q,), lambda r: center[1, q, r] + far[4 + q, r], potential.at[3], edge, other, 3
        )
        local(first, own, lambda r: edge[0, q, r] + first[1, q, r], potential.at[0], second, own, 0)
        local(
            first, other, lambda r: first[0, q, r] + edge[1, q, r], potential.at[1], second, other, 1
        )
        return carry

    lax.fori_loop(0, 4, row, 0)


def spread(parts, lanes):
    total = jnp.concatenate([rows8(parts[k : k + 8]) for k in range(0, len(parts), 8)], 0)
    summed = jnp.sum(total, axis=1, keepdims=True)
    lane = lax.broadcasted_iota(jnp.int32, total.shape, 1)
    return jnp.where(lane == lanes, summed, 0.0)


def start_kernel(flags, near, far, center, own, other, column, first, second, early, late, edge, work):
    lower = flags[0] < 0.5
    pairs = [(own.at[0], own.at[1]), (other.at[4], other.at[5])]
    pairs += [(near.at[8], near.at[9]), (far.at[8], far.at[9])]
    for k, (a, b) in enumerate(pairs):
        a, b = a[...], b[...]
        early[k] = jnp.where(lower, a, b)
        late[k] = jnp.where(lower, b, a)
    two_steps(near, far, center, early, column, first, edge, second, work)


def project(basis, potential, kinds, count):
    def projector(j, total):
        parts = [[None] * 4 for _ in kinds]
        for plane in range(2):
            beta = basis[plane][j]
            wide = None if len(basis) == 2 else basis[2 + plane][j] + potential[plane] * beta
            for k, (field, by) in enumerate(kinds):
                factor = wide if by == "wide" else beta if by is None else by(plane, j, beta)
                for q in range(4):
                    value = fold(field[plane, q] * factor)
                    parts[k][q] = value if plane == 0 else parts[k][q] + value
        flat = [value for part in parts for value in part]
        flat += [jnp.zeros((8, LANES), f32)] * (count - len(flat))
        return total + spread(flat, j)

    return lax.fori_loop(0, PRJ, projector, jnp.zeros((count, LANES), f32))


def share(out, value):
    def copy(k, carry):
        out[k] = value
        return carry

    lax.fori_loop(0, 16, copy, 0)


def split(x):
    high = x.astype(jnp.bfloat16)
    return high, (x - high.astype(f32)).astype(jnp.bfloat16)


def put(target, row, lanes, value, offset):
    high, low = split(value)
    target[row : row + PRJ, lanes] = high
    target[row + offset : row + offset + PRJ, lanes] = low


def flat_rows(ref, s, count):
    return ref[pl.ds(s, count, stride=ROWS)]


def lanes_at(s):
    return pl.ds(pl.multiple_of(s * LANES, LANES), LANES)


def products(a, b):
    return lax.dot_general(a[...], b[...], (((1,), (1,)), ((), ())), preferred_element_type=f32)


def gram_kernel(basis, kinetic, early, late, out, flat):
    def row(s, carry):
        beta, moved = flat_rows(basis, s, PRJ), flat_rows(kinetic, s, PRJ)
        at = lanes_at(s)
        put(flat, 0, at, beta, 64)
        for k, v in enumerate((early, late)):
            put(flat, PRJ * (k + 1), at, moved + v[0, pl.ds(s, 1)] * beta, 64)
        return carry

    for k in (48, 112):
        flat[k : k + PRJ] = jnp.zeros((PRJ, ROWS * LANES), jnp.bfloat16)
    lax.fori_loop(0, ROWS, row, 0, unroll=8)
    both = products(flat, flat)
    both = both[:64] + both[64:]
    both = both + pltpu.roll(both, 64, 1)
    lane = lax.broadcasted_iota(jnp.int32, (PRJ, LANES), 1)
    out[...] = (
        jnp.where((lane >= 16) & (lane < 64), pltpu.roll(both[:16], 16, 1), 0.0)
        + jnp.where((lane >= 64) & (lane < 80), pltpu.roll(both[16:32], 48, 1), 0.0)
        + jnp.where((lane >= 80) & (lane < 96), pltpu.roll(both[32:48], 48, 1), 0.0)
    )


def put_fields(fields, flat):
    def row(s, carry):
        at = lanes_at(s)
        values = [flat_rows(field, s, 8) for field in fields]
        for k in range(0, len(values), 2):
            pair = values[k : k + 2]
            pair = pair if len(pair) == 2 else pair * 2
            put(flat, 8 * k, at, jnp.concatenate(pair, 0), 32)
        return carry

    lax.fori_loop(0, ROWS, row, 0, unroll=8)


def put_basis(own, other, own_k, other_k, potential, flat):
    def row(s, carry):
        at = lanes_at(s)
        for plane, (b, k) in enumerate(((own, own_k), (other, other_k))):
            beta, moved = flat_rows(b, s, PRJ), flat_rows(k, s, PRJ)
            put(flat, 2 * PRJ * plane, at, beta, 64)
            put(flat, 2 * PRJ * plane + PRJ, at, moved + potential[plane, pl.ds(s, 1)] * beta, 64)
        return carry

    lax.fori_loop(0, ROWS, row, 0, unroll=8)


def field_moments(fields_flat, basis_flat, count):
    both = products(fields_flat, basis_flat)
    both = both[:32] + both[32:]
    both = both + pltpu.roll(both, 64, 1)
    result = []
    for k in range(count):
        part = both[8 * k : 8 * k + 8]
        result.append(part + pltpu.roll(pltpu.roll(part, 96, 1), 4, 0))
    return result


def stack_rows(a, b):
    sub = lax.broadcasted_iota(jnp.int32, (8, LANES), 0)
    lane = lax.broadcasted_iota(jnp.int32, (8, LANES), 1)
    return jnp.where(lane < PRJ, jnp.where(sub < 4, a, pltpu.roll(b, 4, 0)), 0.0)


def early_moments_kernel(center, first, second, own, other, out, ahead_flat, fields_flat, basis_flat):
    put_fields((center, first, second), fields_flat)

    def row(s, carry):
        at = lanes_at(s)
        for plane, b in enumerate((own, other)):
            put(basis_flat, 2 * PRJ * plane, at, flat_rows(b, s, PRJ), 64)
        return carry

    for k in (16, 48, 80, 112):
        basis_flat[k : k + PRJ] = jnp.zeros((PRJ, ROWS * LANES), jnp.bfloat16)
    lax.fori_loop(0, ROWS, row, 0, unroll=8)
    found = field_moments(fields_flat, basis_flat, 3)
    out[...] = jnp.concatenate([stack_rows(found[0], found[1]), stack_rows(found[2], 0.0 * found[2])], 0)
    ahead_flat[0:16] = fields_flat[16:32]
    ahead_flat[16:32] = fields_flat[48:64]


def moments_kernel(known, ahead_flat, own, other, own_k, other_k, potential, gram, out, basis_flat):
    def row(s, carry):
        at = lanes_at(s)
        for plane, (b, k) in enumerate(((own, own_k), (other, other_k))):
            wide = flat_rows(k, s, PRJ) + potential[plane, pl.ds(s, 1)] * flat_rows(b, s, PRJ)
            put(basis_flat, PRJ * plane, at, wide, 32)
        return carry

    lax.fori_loop(0, ROWS, row, 0, unroll=8)
    both = products(ahead_flat, basis_flat)
    both = both[:8] + both[16:24]
    both = both[:, :32] + both[:, 32:]
    both = jnp.concatenate([both, jnp.zeros((8, LANES - 32), f32)], 1)
    wide = both + pltpu.roll(pltpu.roll(both, LANES - PRJ, 1), 4, 0)
    moments = jnp.concatenate([known[...][:8], known[...][8:] + stack_rows(0.0 * wide, wide)], 0)
    share(out, moments + gram[...])


def middle_moments_kernel(
    center, potential, own, other, own_k, other_k, wave_x, wave_y, wave_z, out, basis_flat
):
    kinds = [
        (center, None),
        (center, "wide"),
        (center, lambda plane, j, beta: beta * wave_x[plane, j // PRJ_ATOM, 0:1]),
        (center, lambda plane, j, beta: beta * wave_y[j // PRJ_ATOM]),
        (center, lambda plane, j, beta: beta * wave_z[j // PRJ_ATOM]),
    ]
    out[...] = project((own, other, own_k, other_k), potential, kinds, 24)
    flat = [x.reshape(PRJ * ROWS, LANES) for x in (own, other, own_k, other_k)]
    put_basis(*flat, potential, basis_flat)


def second_kernel(
    near, far, center, potential, column, basis_flat, known, first, second, out, edge, work, fields_flat
):
    two_steps(near, far, center, potential, column, first, edge, second, work)
    put_fields([x.reshape(8 * ROWS, LANES) for x in (first, second)], fields_flat)
    found = [pltpu.roll(x, LANES - PRJ, 1) for x in field_moments(fields_flat, basis_flat, 2)]
    value = known[...]
    packed = value[:8] + pltpu.roll(stack_rows(*found), PRJ, 1)
    packed = packed + pltpu.roll(value[8:16], 2 * PRJ, 1) + pltpu.roll(value[16:], 3 * PRJ, 1)
    share(out, packed)


def times_i(x):
    row = lax.broadcasted_iota(jnp.int32, (8, LANES), 0)
    return jnp.where(row < 2, -pltpu.roll(x, 6, 0), pltpu.roll(x, 2, 0))


def coefficients(later, flags, received, strengths, gram):
    upper, sign = flags[0], flags[1]
    sums = []
    for core in range(2):
        acc = received[core]
        for k in range(core + 2, 16, 2):
            acc = acc + received[k]
        sums.append(acc)
    mine = jnp.where(upper > 0.5, sums[1], sums[0])
    if later:
        mine = jnp.concatenate([mine, pltpu.roll(mine, LANES - PRJ, 1)], 0)
    lane = lax.broadcasted_iota(jnp.int32, (PRJ, LANES), 1)
    valid = lane < PRJ
    if later:
        grams = gram[...]
    else:
        theirs = jnp.where(upper > 0.5, sums[0], sums[1])
        turned = jnp.where(
            (lane >= 48) & (lane < 64) | (lane >= 80),
            pltpu.roll(theirs, PRJ, 1),
            pltpu.roll(theirs, LANES - PRJ, 1),
        )
        grams = mine + jnp.where(lane < 32, theirs, turned)
        gram[...] = grams

    def block(k):
        return jnp.where(valid, pltpu.roll(grams, LANES - PRJ * (k + 1), 1), 0.0)

    g0 = block(0)
    g1, g2 = (block(2), block(4)) if later else (block(1), block(3))
    weight = strengths[...]

    def moment(k):
        rolled = mine if k == 0 else pltpu.roll(mine, PRJ - 4 * k, 0)
        return jnp.where(valid, rolled, 0.0)[:8]

    def apply(c, g):
        return jnp.dot(c[:, :PRJ], g, precision=highest, preferred_element_type=f32)

    c0 = weight * moment(0)
    c1 = weight * (moment(1) + apply(c0, g0))
    c2 = weight * (moment(2) + apply(c0, g1) + apply(c1, g0))
    c3 = weight * (moment(3) + apply(c0, g2) + apply(c1, g1) + apply(c2, g0))
    e0 = times_i((sign * half_step) * c0 + (sign * A3) * c2) + A2 * c1 + A4 * c3
    e1 = A2 * c0 + A4 * c2
    return c0, c1, e0, e1


def spread_table(table, sets):
    row = lax.broadcasted_iota(jnp.int32, (PRJ, LANES), 0)
    lane = lax.broadcasted_iota(jnp.int32, (PRJ, LANES), 1)
    for k, c in enumerate(sets):
        for q in range(4):
            wide = jnp.broadcast_to(c[q : q + 1], (PRJ, LANES))
            column = jnp.sum(jnp.where(row == lane, wide, 0.0), axis=1, keepdims=True)
            for j in range(PRJ):
                table[j, k, q] = jnp.broadcast_to(column[j : j + 1], (8, LANES))


def combine(out, start, basis, potential, table):
    def tile(i, carry):
        rows = pl.ds(pl.multiple_of(i * 8, 8), 8)
        for plane in range(2):
            v = potential[plane, rows]
            total = start(plane, rows)
            for j in range(PRJ):
                beta = basis[plane][j, rows]
                wide = basis[2 + plane][j, rows] + v * beta
                for q in range(4):
                    total[q] = total[q] + table[j, 0, q] * wide + table[j, 1, q] * beta
            for q in range(4):
                out[plane, q, rows] = total[q]
        return carry

    lax.fori_loop(0, ROWS // 8, tile, 0)


def advance_kernel(later, flags, received, strengths, second, own, other, own_k, other_k, potential, *refs):
    if later:
        gram, out, rest, table = refs
    else:
        out, rest, gram, table = refs
    c0, c1, e0, e1 = coefficients(later, flags, received, strengths, gram)
    rest[0] = e1
    rest[1] = e0
    spread_table(table, (c0, c1))

    def start(plane, rows):
        return [second[plane, q, rows] for q in range(4)]

    combine(out, start, (own, other, own_k, other_k), potential, table)


def partial_kernel(flags, center, first, second, own, other, own_k, other_k, potential, rest, out, table):
    sign = flags[1]
    spread_table(table, (rest[0], rest[1]))

    def start(plane, rows):
        moved = [first[plane, q, rows] for q in range(4)]
        mixed = [-moved[2], -moved[3], moved[0], moved[1]]
        return [
            center[plane, q, rows] + (sign * half_step) * mixed[q] + A2 * second[plane, q, rows]
            for q in range(4)
        ]

    combine(out, start, (own, other, own_k, other_k), potential, table)


def last_kernel(flags, near, far, center, potential, column, partial, out, first, edge, second, work):
    two_steps(near, far, center, potential, column, first, edge, second, work)
    sign = flags[1]
    for plane in range(2):
        for q in range(4):
            mixed = -first[plane, q + 2] if q < 2 else first[plane, q - 2]
            out[plane, q] = partial[plane, q] + (sign * A3) * mixed + A4 * second[plane, q]


def payload_kernel(flags, mine, yours, received, strengths, out):
    turned = [mine[0, q] * yours[q + 2] - mine[0, q + 2] * yours[q] for q in range(2)]
    density = (-2.0 * half_step * flags[1]) * (turned[0] + turned[1])
    sums = []
    for core in range(2):
        acc = received[core]
        for k in range(core + 2, 16, 2):
            acc = acc + received[k]
        sums.append(acc)
    forces = []
    for q in range(3):
        rows, shift = slice(4 * (q % 2), 4 * (q % 2) + 4), LANES - (2 + q // 2) * PRJ
        slopes = [pltpu.roll(x, shift, 1)[rows] for x in sums]
        products = sums[0][:4] * slopes[1] + sums[1][:4] * slopes[0]
        forces.append(strengths[...] * jnp.sum(products, axis=0, keepdims=True))
    for k in range(16):
        first = 9 * k // 2
        out[k] = jnp.concatenate([density[first : first + 5]] + forces, 0)


def outcome_kernel(odd, received, density, forces):
    total = received[0]
    for k in range(1, 16):
        total = total + received[k]
    lane = lax.broadcasted_iota(jnp.int32, (1, LANES), 1)
    moved = pltpu.roll(total, 64, 1)
    for k in range(5):
        start = total[k : k + 1]
        shifted = jnp.where(lane < 64, moved[k : k + 1], moved[min(k + 1, 4) : min(k + 1, 4) + 1])
        row = jnp.where(odd[0] > 0, shifted, start)
        width = min(LANES, 576 - k * LANES)
        density[:, k * LANES : k * LANES + width] = row[:, :width]
    atom = lax.broadcasted_iota(jnp.int32, (3, LANES), 1) // PRJ_ATOM
    column = lax.broadcasted_iota(jnp.int32, (3, 4), 1)
    result = jnp.zeros((3, 4), f32)
    for a in range(4):
        part = jnp.sum(jnp.where(atom == a, total[5:8], 0.0), axis=1, keepdims=True)
        result = jnp.where(column == a, part * (1.0 / NB), result)
    forces[...] = result


def swap_core(x):
    return lax.ppermute(x, "space", [(i, i ^ 1) for i in range(16)])


def fence(*values):
    return lax.optimization_barrier(values)


def body(
    psi_start,
    adjoint_end,
    potential_now,
    potential_next,
    projector_tiles,
    tile_map,
    strengths,
    positions,
):
    space, band = lax.axis_index("space"), lax.axis_index("band")
    lower = (space % 2) == 0
    column = jnp.asarray(columns())
    plane_shape = (ROWS, LANES)
    fields_shape = (2, 4) + plane_shape
    rows_shape = (PRJ,) + plane_shape
    flags = jnp.stack([jnp.where(lower, 0.0, 1.0), jnp.where(lower, -1.0, 1.0)]).astype(f32)
    atom = (band // PRJ_ATOM).astype(jnp.int32).reshape(1)
    odd = (band % 2).astype(jnp.int32).reshape(1)

    payload = call(
        mask_kernel,
        rows_shape,
        [atom, projector_tiles.reshape(plane_shape), tile_map.reshape(4, ROWS)],
        scalars=1,
    )
    basis_own = lax.all_to_all(payload, "band", 0, 0, tiled=True)

    kept, given, own = call(
        give_kernel,
        [(4,) + plane_shape, (6,) + plane_shape, (2,) + plane_shape],
        [
            flags,
            psi_start.reshape((4,) + plane_shape),
            adjoint_end.reshape((4,) + plane_shape),
            potential_now.reshape(plane_shape),
            potential_next.reshape(plane_shape),
        ],
        scalars=1,
    )
    other = swap_core(given)
    near_message, far_message, center = call(
        pack_kernel,
        [(10,) + plane_shape, (10,) + plane_shape, fields_shape],
        [kept, own, other],
    )

    from_near = [(i, (i + 2) % 16 if i % 2 == 0 else (i - 2) % 16) for i in range(16)]
    from_far = [(j, i) for i, j in from_near]
    beside = [(i, (i + 1) % 16 if i % 2 else (i - 1) % 16) for i in range(16)]

    def exchange(fields):
        flat = fields.reshape((8,) + plane_shape)
        return (lax.ppermute(flat, "space", from_near), lax.ppermute(flat, "space", from_far))

    near = lax.ppermute(near_message, "space", from_near)
    far = lax.ppermute(far_message, "space", from_far)

    basis_own, near, far, strengths, positions = fence(
        basis_own, near, far, strengths, positions
    )
    basis_near = lax.ppermute(basis_own, "space", beside)
    basis_other = swap_core(basis_own)

    field_scratch = pltpu.VMEM(fields_shape, f32)
    work_scratch = pltpu.VMEM((4, 3) + plane_shape, f32)
    first, second, early, late = call(
        start_kernel,
        [fields_shape, fields_shape, (4,) + plane_shape, (4,) + plane_shape],
        [flags, near, far, center, own, other, column],
        scratch=[field_scratch, work_scratch],
        scalars=1,
    )
    flat_shape = (PRJ * ROWS, LANES)
    fields_flat = (8 * ROWS, LANES)
    known, ahead_flat = call(
        early_moments_kernel,
        [(16, LANES), jax.ShapeDtypeStruct((32, ROWS * LANES), jnp.bfloat16)],
        [x.reshape(fields_flat) for x in (center, first, second)]
        + [x.reshape(flat_shape) for x in (basis_own, basis_other)],
        scratch=[
            pltpu.VMEM((64, ROWS * LANES), jnp.bfloat16),
            pltpu.VMEM((128, ROWS * LANES), jnp.bfloat16),
        ],
        mib=12,
    )
    basis_near, first, second, early, late, known = fence(
        basis_near, first, second, early, late, known
    )
    kinetic_own = call(
        kinetic_kernel,
        rows_shape,
        [basis_own, basis_other, basis_near, column],
        scratch=[work_scratch],
    )
    kinetic_other = swap_core(kinetic_own)
    gram_part = call(
        gram_kernel,
        (PRJ, LANES),
        [basis_own.reshape(flat_shape), kinetic_own.reshape(flat_shape), early, late],
        scratch=[pltpu.VMEM((128, ROWS * LANES), jnp.bfloat16)],
        mib=12,
    )
    kinetic_other, gram_part = fence(kinetic_other, gram_part)
    basis = [basis_own, basis_other, kinetic_own, kinetic_other]
    part = call(
        moments_kernel,
        (16, 16, LANES),
        [known, ahead_flat] + [x.reshape(flat_shape) for x in basis] + [early, gram_part],
        scratch=[pltpu.VMEM((64, ROWS * LANES), jnp.bfloat16)],
        mib=12,
    )

    table_scratch = pltpu.VMEM((PRJ, 2, 4, 8, LANES), f32)
    rest_shape = (2, 8, LANES)
    received = lax.all_to_all(part, "space", 0, 0, tiled=True)
    received, strengths, positions, space, first, second, early, late, center = fence(
        received, strengths, positions, space, first, second, early, late, center
    )
    plane = space + jnp.stack([jnp.int32(0), 1 - 2 * (space % 2)])
    flat = np.arange(ROWS * LANES, dtype=np.int32)
    wave_x = jnp.sin(
        2.0 * math.pi / 16 * (plane[:, None] - positions[0][None, :]).astype(f32)
    )
    wave_x = jnp.broadcast_to(wave_x[:, :, None, None], (2, 4, 8, LANES))
    wave_y = jnp.sin(
        2.0 * math.pi / NY * (jnp.asarray(flat // NZ)[None, :] - positions[1][:, None]).astype(f32)
    ).reshape((4,) + plane_shape)
    wave_z = jnp.sin(
        2.0 * math.pi / NZ * (jnp.asarray(flat % NZ)[None, :] - positions[2][:, None]).astype(f32)
    ).reshape((4,) + plane_shape)
    weight = jnp.pad(strengths, (0, LANES - PRJ)).reshape(1, LANES)
    u2, rest, gram = call(
        functools.partial(advance_kernel, False),
        [fields_shape, rest_shape, (PRJ, LANES)],
        [flags, received, weight, second] + basis + [early],
        scratch=[table_scratch],
        scalars=1,
    )

    def finish(center, first, second, around, u2, rest, parts=None):
        flat = u2.reshape((8,) + plane_shape)
        near = lax.ppermute(flat, "space", from_near)
        shared = None
        if parts is not None:
            flat, parts = fence(flat, parts)
            far = lax.ppermute(flat, "space", from_far)
            shared = lax.all_to_all(parts, "band", 0, 0, tiled=True)
            rest, shared = fence(rest, shared)
        partial = call(
            partial_kernel,
            fields_shape,
            [flags, center, first, second] + basis + [around, rest],
            scratch=[table_scratch],
            scalars=1,
        )
        if parts is None:
            flat, partial = fence(flat, partial)
            far = lax.ppermute(flat, "space", from_far)
        return shared, call(
            last_kernel,
            fields_shape,
            [flags, near, far, u2, around, column, partial],
            scratch=[field_scratch] * 3 + [work_scratch],
            scalars=1,
        )

    _, mid = finish(center, first, second, early, u2, rest)
    near, far = exchange(mid)
    yours = swap_core(mid[1])
    known, basis_flat = call(
        middle_moments_kernel,
        [(24, LANES), jax.ShapeDtypeStruct((128, ROWS * LANES), jnp.bfloat16)],
        [mid, late] + basis + [wave_x, wave_y, wave_z],
    )
    first, second, part = call(
        second_kernel,
        [fields_shape, fields_shape, (16, 8, LANES)],
        [near, far, mid, late, column, basis_flat, known],
        scratch=[
            field_scratch,
            work_scratch,
            pltpu.VMEM((64, ROWS * LANES), jnp.bfloat16),
        ],
    )
    part, yours = fence(part, yours)
    received = lax.all_to_all(part, "space", 0, 0, tiled=True)
    received, first, second, late, mid, yours = fence(received, first, second, late, mid, yours)
    u2, rest = call(
        functools.partial(advance_kernel, True),
        [fields_shape, rest_shape],
        [flags, received, weight, second] + basis + [late, gram],
        scratch=[table_scratch],
        scalars=1,
    )

    u2, yours = fence(u2, yours)
    parts = call(
        payload_kernel, (16, 8, LANES), [flags, mid, yours, received, weight], scalars=1
    )
    shared, end = finish(mid, first, second, late, u2, rest, parts)
    density, forces = call(outcome_kernel, [(1, 576), (3, 4)], [odd, shared], scalars=1)

    swapped = swap_core(end[1])
    psi_end = jnp.where(lower, end[0], swapped).reshape(psi_start.shape)
    adjoint_start = jnp.where(lower, swapped, end[0]).reshape(adjoint_end.shape)
    return (psi_end, adjoint_start, density, forces)


def solution(mesh):
    return jax.shard_map(
        body,
        mesh=mesh,
        in_specs=(
            P(None, "band", "space", None),
            P(None, "band", "space", None),
            P("space", None),
            P("space", None),
            P("band", "space", None),
            P(None, "space", None),
            P(),
            P(),
        ),
        out_specs=(
            P(None, "band", "space", None),
            P(None, "band", "space", None),
            P("space", "band"),
            P(),
        ),
        check_vma=False,
    )
```

```python
import functools
import math

import jax
import jax.numpy as jnp
import numpy as np
from jax import lax
from jax.experimental import pallas as pl
from jax.experimental.pallas import tpu as pltpu
from jax.sharding import PartitionSpec as P

NB = 32
NY = 96
NZ = 96
ROWS = 72
LANES = 128
PRJ = 16
PRJ_ATOM = 4

half_step = 0.025
kinetic_scale = 3.125
highest = lax.Precision.HIGHEST
f32 = jnp.float32

A2 = -(half_step**2) / 2.0
A3 = -(half_step**3) / 6.0
A4 = half_step**4 / 24.0


def columns():
    return (np.arange(ROWS * LANES, dtype=np.int32) % NZ).reshape(ROWS, LANES)


TILES = [slice(8 * t, 8 * t + 8) for t in range(ROWS // 8)]


def next_rows(ref, index, t, x, sub):
    if t < len(TILES) - 1:
        return ref[index + (slice(8 * t + 1, 8 * t + 9),)]
    wrapped = jnp.broadcast_to(ref[index + (slice(0, 1),)], (8, LANES))
    return jnp.where(sub == 7, wrapped, pltpu.roll(x, 7, 0))


def previous_rows(ref, index, t, x, sub):
    if t > 0:
        return ref[index + (slice(8 * t - 1, 8 * t + 7),)]
    wrapped = jnp.broadcast_to(ref[index + (slice(ROWS - 1, ROWS),)], (8, LANES))
    return jnp.where(sub == 0, wrapped, pltpu.roll(x, 1, 0))


def around_plane(ref, index, column, store, scratch):
    lane = lax.broadcasted_iota(jnp.int32, (8, LANES), 1)
    sub = lax.broadcasted_iota(jnp.int32, (8, LANES), 0)
    for t, rows in enumerate(TILES):
        x = ref[index + (rows,)]
        after, before = next_rows(ref, index, t, x, sub), previous_rows(ref, index, t, x, sub)
        up = pltpu.roll(jnp.where(lane >= 96, x, after), 32, 1)
        down = pltpu.roll(jnp.where(lane < 32, x, before), 96, 1)
        place = column[rows]
        scratch[0, rows] = up + down
        scratch[1, rows] = jnp.where(place == 0, down, x)
        scratch[2, rows] = jnp.where(place == NZ - 1, up, x)
    for t, rows in enumerate(TILES):
        ahead, behind = scratch[1, rows], scratch[2, rows]
        after = next_rows(scratch, (1,), t, ahead, sub)
        before = previous_rows(scratch, (2,), t, behind, sub)
        up = pltpu.roll(jnp.where(lane >= 1, ahead, after), 127, 1)
        down = pltpu.roll(jnp.where(lane < 127, behind, before), 1, 1)
        store(rows, scratch[0, rows] + (up + down))


def fold(x):
    return jnp.sum(x.reshape(ROWS // 8, 8, LANES), axis=0)


def rows8(parts):
    sub = lax.broadcasted_iota(jnp.int32, (8, LANES), 0)
    low = sub < 4
    parts = [
        jnp.where(low, a, b) + pltpu.roll(jnp.where(low, b, a), 4, 0)
        for a, b in zip(parts[:4], parts[4:])
    ]
    for step in (2, 1):
        first = (sub & step) == 0
        parts = [
            jnp.where(first, a + pltpu.roll(a, 8 - step, 0), b + pltpu.roll(b, step, 0))
            for a, b in zip(parts[:step], parts[step:])
        ]
    return parts[0]


def params(mib):
    return pltpu.CompilerParams(vmem_limit_bytes=mib * 2**20)


VMEM = pl.BlockSpec(memory_space=pltpu.VMEM)
SMEM = pl.BlockSpec(memory_space=pltpu.SMEM)


def call(kernel, outs, args, scratch=(), scalars=0, mib=8, cost=None):
    specs = [SMEM] * scalars + [VMEM] * (len(args) - scalars)
    single = not isinstance(outs, list)
    shapes = [
        o if hasattr(o, "dtype") else jax.ShapeDtypeStruct(o, f32)
        for o in ([outs] if single else outs)
    ]
    result = pl.pallas_call(
        kernel,
        out_shape=shapes,
        in_specs=specs,
        out_specs=[VMEM] * len(shapes),
        scratch_shapes=list(scratch),
        compiler_params=params(mib),
        cost_estimate=cost,
    )(*args)
    return result[0] if single else result


def mask_kernel(atom, values, tile_map, out):
    reach = tile_map[pl.ds(atom[0], 1)].astype(f32)
    row = lax.broadcasted_iota(jnp.int32, (ROWS, ROWS), 0)
    lane = lax.broadcasted_iota(jnp.int32, (ROWS, ROWS), 1)
    wide = jnp.where(row == lane, jnp.broadcast_to(reach, (ROWS, ROWS)), 0.0)
    share(out, values[...] * jnp.sum(wide, axis=1, keepdims=True))


def give_kernel(flags, psi, adjoint, now, later, kept, message, own):
    lower = flags[0] < 0.5
    for q in range(4):
        a, b = psi[q], adjoint[q]
        kept[q] = jnp.where(lower, a, b)
        message[q] = jnp.where(lower, b, a)
    own[0] = now[...]
    own[1] = later[...]
    message[4] = now[...]
    message[5] = later[...]


def pack_kernel(kept, own, other, near, far, center):
    center[0] = kept[...]
    center[1] = other[0:4]
    near[0:4] = kept[...]
    near[4:10] = other[...]
    far[0:4] = kept[...]
    far[4:8] = other[0:4]
    far[8:10] = own[...]


def kinetic_kernel(basis, basis_other, basis_near, column, out, work):
    def projector(pair, carry):
        for k in range(2):
            j = 2 * pair + k

            def store(rows, around):
                beside = basis_other[j, rows] + basis_near[j, rows]
                out[j, rows] = kinetic_scale * (6.0 * basis[j, rows] - around - beside)

            around_plane(basis, (j,), column, store, work.at[k])
        return carry

    lax.fori_loop(0, PRJ // 2, projector, 0)


def two_steps(near, far, center, potential, column, first, mixed, second, work):
    def row(q, carry):
        sides = [(0, 1, near, 4 + q, q), (1, 0, far, q, 4 + q)]
        for plane, across, message, edge, beyond in sides:

            def store(r, around, plane=plane, across=across, message=message, edge=edge):
                x, e = center[plane, q, r], message[edge, r]
                value = kinetic_scale * (6.0 * x - around - (e + center[across, q, r]))
                value = value + potential[plane, r] * x
                first[plane, q, r] = value
                mixed[plane, q, r] = value - kinetic_scale * e

            around_plane(center, (plane, q), column, store, work.at[plane])
        for plane, across, message, edge, beyond in sides:

            def store(r, around, plane=plane, across=across, message=message, edge=edge, beyond=beyond):
                f, e = first[plane, q, r], message[edge, r]
                beside = kinetic_scale * (6.0 * e - message[beyond, r] - center[plane, q, r])
                beside = beside + potential[2 + plane, r] * e + first[across, q, r]
                value = kinetic_scale * (6.0 * f - around - beside)
                second[plane, q, r] = value + potential[plane, r] * f

            around_plane(mixed, (plane, q), column, store, work.at[2 + plane])
        return carry

    lax.fori_loop(0, 4, row, 0)


def spread(parts, lanes):
    total = jnp.concatenate([rows8(parts[k : k + 8]) for k in range(0, len(parts), 8)], 0)
    summed = jnp.sum(total, axis=1, keepdims=True)
    lane = lax.broadcasted_iota(jnp.int32, total.shape, 1)
    return jnp.where(lane == lanes, summed, 0.0)


def start_kernel(flags, near, far, center, own, other, column, first, second, early, late, edge, work):
    lower = flags[0] < 0.5
    pairs = [(own.at[0], own.at[1]), (other.at[4], other.at[5])]
    pairs += [(near.at[8], near.at[9]), (far.at[8], far.at[9])]
    for k, (a, b) in enumerate(pairs):
        a, b = a[...], b[...]
        early[k] = jnp.where(lower, a, b)
        late[k] = jnp.where(lower, b, a)
    two_steps(near, far, center, early, column, first, edge, second, work)


def project(basis, potential, kinds, count):
    def projector(j, total):
        parts = [[None] * 4 for _ in kinds]
        for plane in range(2):
            beta = basis[plane][j]
            wide = None if len(basis) == 2 else basis[2 + plane][j] + potential[plane] * beta
            for k, (field, by) in enumerate(kinds):
                factor = wide if by == "wide" else beta if by is None else by(plane, j, beta)
                for q in range(4):
                    value = fold(field[plane, q] * factor)
                    parts[k][q] = value if plane == 0 else parts[k][q] + value
        flat = [value for part in parts for value in part]
        flat += [jnp.zeros((8, LANES), f32)] * (count - len(flat))
        return total + spread(flat, j)

    return lax.fori_loop(0, PRJ, projector, jnp.zeros((count, LANES), f32))


def share(out, value):
    def copy(k, carry):
        out[k] = value
        return carry

    lax.fori_loop(0, 16, copy, 0)


def split(x):
    high = x.astype(jnp.bfloat16)
    return high, (x - high.astype(f32)).astype(jnp.bfloat16)


def put(target, row, lanes, value, offset):
    high, low = split(value)
    target[row : row + PRJ, lanes] = high
    target[row + offset : row + offset + PRJ, lanes] = low


def flat_rows(ref, s, count):
    return ref[pl.ds(s, count, stride=ROWS)]


def lanes_at(s):
    return pl.ds(pl.multiple_of(s * LANES, LANES), LANES)


def products(a, b):
    return lax.dot_general(a[...], b[...], (((1,), (1,)), ((), ())), preferred_element_type=f32)


def gram_kernel(basis, kinetic, early, late, out, flat):
    def row(s, carry):
        beta, moved = flat_rows(basis, s, PRJ), flat_rows(kinetic, s, PRJ)
        at = lanes_at(s)
        put(flat, 0, at, beta, 64)
        for k, v in enumerate((early, late)):
            put(flat, PRJ * (k + 1), at, moved + v[0, pl.ds(s, 1)] * beta, 64)
        return carry

    for k in (48, 112):
        flat[k : k + PRJ] = jnp.zeros((PRJ, ROWS * LANES), jnp.bfloat16)
    lax.fori_loop(0, ROWS, row, 0, unroll=8)
    both = products(flat, flat)
    both = both[:64] + both[64:]
    both = both + pltpu.roll(both, 64, 1)
    lane = lax.broadcasted_iota(jnp.int32, (PRJ, LANES), 1)
    out[...] = (
        jnp.where((lane >= 16) & (lane < 64), pltpu.roll(both[:16], 16, 1), 0.0)
        + jnp.where((lane >= 64) & (lane < 80), pltpu.roll(both[16:32], 48, 1), 0.0)
        + jnp.where((lane >= 80) & (lane < 96), pltpu.roll(both[32:48], 48, 1), 0.0)
    )


def put_fields(fields, flat):
    def row(s, carry):
        at = lanes_at(s)
        values = [flat_rows(field, s, 8) for field in fields]
        for k in range(0, len(values), 2):
            pair = values[k : k + 2]
            pair = pair if len(pair) == 2 else pair * 2
            put(flat, 8 * k, at, jnp.concatenate(pair, 0), 32)
        return carry

    lax.fori_loop(0, ROWS, row, 0, unroll=8)


def put_basis(own, other, own_k, other_k, potential, flat):
    def row(s, carry):
        at = lanes_at(s)
        for plane, (b, k) in enumerate(((own, own_k), (other, other_k))):
            beta, moved = flat_rows(b, s, PRJ), flat_rows(k, s, PRJ)
            put(flat, 2 * PRJ * plane, at, beta, 64)
            put(flat, 2 * PRJ * plane + PRJ, at, moved + potential[plane, pl.ds(s, 1)] * beta, 64)
        return carry

    lax.fori_loop(0, ROWS, row, 0, unroll=8)


def field_moments(fields_flat, basis_flat, count):
    both = products(fields_flat, basis_flat)
    both = both[:32] + both[32:]
    both = both + pltpu.roll(both, 64, 1)
    result = []
    for k in range(count):
        part = both[8 * k : 8 * k + 8]
        result.append(part + pltpu.roll(pltpu.roll(part, 96, 1), 4, 0))
    return result


def stack_rows(a, b):
    sub = lax.broadcasted_iota(jnp.int32, (8, LANES), 0)
    lane = lax.broadcasted_iota(jnp.int32, (8, LANES), 1)
    return jnp.where(lane < PRJ, jnp.where(sub < 4, a, pltpu.roll(b, 4, 0)), 0.0)


def early_moments_kernel(center, first, second, own, other, out, ahead_flat, fields_flat, basis_flat):
    put_fields((center, first, second), fields_flat)

    def row(s, carry):
        at = lanes_at(s)
        for plane, b in enumerate((own, other)):
            put(basis_flat, 2 * PRJ * plane, at, flat_rows(b, s, PRJ), 64)
        return carry

    for k in (16, 48, 80, 112):
        basis_flat[k : k + PRJ] = jnp.zeros((PRJ, ROWS * LANES), jnp.bfloat16)
    lax.fori_loop(0, ROWS, row, 0, unroll=8)
    found = field_moments(fields_flat, basis_flat, 3)
    out[...] = jnp.concatenate([stack_rows(found[0], found[1]), stack_rows(found[2], 0.0 * found[2])], 0)
    ahead_flat[0:16] = fields_flat[16:32]
    ahead_flat[16:32] = fields_flat[48:64]


def moments_kernel(known, ahead_flat, own, other, own_k, other_k, potential, gram, out, basis_flat):
    def row(s, carry):
        at = lanes_at(s)
        for plane, (b, k) in enumerate(((own, own_k), (other, other_k))):
            wide = flat_rows(k, s, PRJ) + potential[plane, pl.ds(s, 1)] * flat_rows(b, s, PRJ)
            put(basis_flat, PRJ * plane, at, wide, 32)
        return carry

    lax.fori_loop(0, ROWS, row, 0, unroll=8)
    both = products(ahead_flat, basis_flat)
    both = both[:8] + both[16:24]
    both = both[:, :32] + both[:, 32:]
    both = jnp.concatenate([both, jnp.zeros((8, LANES - 32), f32)], 1)
    wide = both + pltpu.roll(pltpu.roll(both, LANES - PRJ, 1), 4, 0)
    moments = jnp.concatenate([known[...][:8], known[...][8:] + stack_rows(0.0 * wide, wide)], 0)
    share(out, moments + gram[...])


def middle_moments_kernel(
    center, potential, own, other, own_k, other_k, wave_x, wave_y, wave_z, out, basis_flat
):
    kinds = [
        (center, None),
        (center, "wide"),
        (center, lambda plane, j, beta: beta * wave_x[plane, j // PRJ_ATOM, 0:1]),
        (center, lambda plane, j, beta: beta * wave_y[j // PRJ_ATOM]),
        (center, lambda plane, j, beta: beta * wave_z[j // PRJ_ATOM]),
    ]
    out[...] = project((own, other, own_k, other_k), potential, kinds, 24)
    flat = [x.reshape(PRJ * ROWS, LANES) for x in (own, other, own_k, other_k)]
    put_basis(*flat, potential, basis_flat)


def second_kernel(
    near, far, center, potential, column, basis_flat, known, first, second, out, edge, work, fields_flat
):
    two_steps(near, far, center, potential, column, first, edge, second, work)
    put_fields([x.reshape(8 * ROWS, LANES) for x in (first, second)], fields_flat)
    found = [pltpu.roll(x, LANES - PRJ, 1) for x in field_moments(fields_flat, basis_flat, 2)]
    value = known[...]
    packed = value[:8] + pltpu.roll(stack_rows(*found), PRJ, 1)
    packed = packed + pltpu.roll(value[8:16], 2 * PRJ, 1) + pltpu.roll(value[16:], 3 * PRJ, 1)
    share(out, packed)


def times_i(x):
    row = lax.broadcasted_iota(jnp.int32, (8, LANES), 0)
    return jnp.where(row < 2, -pltpu.roll(x, 6, 0), pltpu.roll(x, 2, 0))


def coefficients(later, flags, received, strengths, gram):
    upper, sign = flags[0], flags[1]
    sums = []
    for core in range(2):
        acc = received[core]
        for k in range(core + 2, 16, 2):
            acc = acc + received[k]
        sums.append(acc)
    mine = jnp.where(upper > 0.5, sums[1], sums[0])
    if later:
        mine = jnp.concatenate([mine, pltpu.roll(mine, LANES - PRJ, 1)], 0)
    lane = lax.broadcasted_iota(jnp.int32, (PRJ, LANES), 1)
    valid = lane < PRJ
    if later:
        grams = gram[...]
    else:
        theirs = jnp.where(upper > 0.5, sums[0], sums[1])
        turned = jnp.where(
            (lane >= 48) & (lane < 64) | (lane >= 80),
            pltpu.roll(theirs, PRJ, 1),
            pltpu.roll(theirs, LANES - PRJ, 1),
        )
        grams = mine + jnp.where(lane < 32, theirs, turned)
        gram[...] = grams

    def block(k):
        return jnp.where(valid, pltpu.roll(grams, LANES - PRJ * (k + 1), 1), 0.0)

    g0 = block(0)
    g1, g2 = (block(2), block(4)) if later else (block(1), block(3))
    weight = strengths[...]

    def moment(k):
        rolled = mine if k == 0 else pltpu.roll(mine, PRJ - 4 * k, 0)
        return jnp.where(valid, rolled, 0.0)[:8]

    def apply(c, g):
        return jnp.dot(c[:, :PRJ], g, precision=highest, preferred_element_type=f32)

    c0 = weight * moment(0)
    c1 = weight * (moment(1) + apply(c0, g0))
    c2 = weight * (moment(2) + apply(c0, g1) + apply(c1, g0))
    c3 = weight * (moment(3) + apply(c0, g2) + apply(c1, g1) + apply(c2, g0))
    e0 = times_i((sign * half_step) * c0 + (sign * A3) * c2) + A2 * c1 + A4 * c3
    e1 = A2 * c0 + A4 * c2
    return c0, c1, e0, e1


def spread_table(table, sets):
    row = lax.broadcasted_iota(jnp.int32, (PRJ, LANES), 0)
    lane = lax.broadcasted_iota(jnp.int32, (PRJ, LANES), 1)
    for k, c in enumerate(sets):
        for q in range(4):
            wide = jnp.broadcast_to(c[q : q + 1], (PRJ, LANES))
            column = jnp.sum(jnp.where(row == lane, wide, 0.0), axis=1, keepdims=True)
            for j in range(PRJ):
                table[j, k, q] = jnp.broadcast_to(column[j : j + 1], (8, LANES))


def combine(out, start, basis, potential, table):
    def tile(i, carry):
        rows = pl.ds(pl.multiple_of(i * 8, 8), 8)
        for plane in range(2):
            v = potential[plane, rows]
            total = start(plane, rows)
            for j in range(PRJ):
                beta = basis[plane][j, rows]
                wide = basis[2 + plane][j, rows] + v * beta
                for q in range(4):
                    total[q] = total[q] + table[j, 0, q] * wide + table[j, 1, q] * beta
            for q in range(4):
                out[plane, q, rows] = total[q]
        return carry

    lax.fori_loop(0, ROWS // 8, tile, 0)


def advance_kernel(later, flags, received, strengths, second, own, other, own_k, other_k, potential, *refs):
    if later:
        gram, out, rest, table = refs
    else:
        out, rest, gram, table = refs
    c0, c1, e0, e1 = coefficients(later, flags, received, strengths, gram)
    rest[0] = e1
    rest[1] = e0
    spread_table(table, (c0, c1))

    def start(plane, rows):
        return [second[plane, q, rows] for q in range(4)]

    combine(out, start, (own, other, own_k, other_k), potential, table)


def partial_kernel(flags, center, first, second, own, other, own_k, other_k, potential, rest, out, table):
    sign = flags[1]
    spread_table(table, (rest[0], rest[1]))

    def start(plane, rows):
        moved = [first[plane, q, rows] for q in range(4)]
        mixed = [-moved[2], -moved[3], moved[0], moved[1]]
        return [
            center[plane, q, rows] + (sign * half_step) * mixed[q] + A2 * second[plane, q, rows]
            for q in range(4)
        ]

    combine(out, start, (own, other, own_k, other_k), potential, table)


def last_kernel(flags, near, far, center, potential, column, partial, out, first, edge, second, work):
    two_steps(near, far, center, potential, column, first, edge, second, work)
    sign = flags[1]
    for plane in range(2):
        for q in range(4):
            mixed = -first[plane, q + 2] if q < 2 else first[plane, q - 2]
            out[plane, q] = partial[plane, q] + (sign * A3) * mixed + A4 * second[plane, q]


def payload_kernel(flags, mine, yours, received, strengths, out):
    turned = [mine[0, q] * yours[q + 2] - mine[0, q + 2] * yours[q] for q in range(2)]
    density = (-2.0 * half_step * flags[1]) * (turned[0] + turned[1])
    sums = []
    for core in range(2):
        acc = received[core]
        for k in range(core + 2, 16, 2):
            acc = acc + received[k]
        sums.append(acc)
    forces = []
    for q in range(3):
        rows, shift = slice(4 * (q % 2), 4 * (q % 2) + 4), LANES - (2 + q // 2) * PRJ
        slopes = [pltpu.roll(x, shift, 1)[rows] for x in sums]
        products = sums[0][:4] * slopes[1] + sums[1][:4] * slopes[0]
        forces.append(strengths[...] * jnp.sum(products, axis=0, keepdims=True))
    for k in range(16):
        first = 9 * k // 2
        out[k] = jnp.concatenate([density[first : first + 5]] + forces, 0)


def outcome_kernel(odd, received, density, forces):
    total = received[0]
    for k in range(1, 16):
        total = total + received[k]
    lane = lax.broadcasted_iota(jnp.int32, (1, LANES), 1)
    moved = pltpu.roll(total, 64, 1)
    for k in range(5):
        start = total[k : k + 1]
        shifted = jnp.where(lane < 64, moved[k : k + 1], moved[min(k + 1, 4) : min(k + 1, 4) + 1])
        row = jnp.where(odd[0] > 0, shifted, start)
        width = min(LANES, 576 - k * LANES)
        density[:, k * LANES : k * LANES + width] = row[:, :width]
    atom = lax.broadcasted_iota(jnp.int32, (3, LANES), 1) // PRJ_ATOM
    column = lax.broadcasted_iota(jnp.int32, (3, 4), 1)
    result = jnp.zeros((3, 4), f32)
    for a in range(4):
        part = jnp.sum(jnp.where(atom == a, total[5:8], 0.0), axis=1, keepdims=True)
        result = jnp.where(column == a, part * (1.0 / NB), result)
    forces[...] = result


def swap_core(x):
    return lax.ppermute(x, "space", [(i, i ^ 1) for i in range(16)])


def fence(*values):
    return lax.optimization_barrier(values)


def body(
    psi_start,
    adjoint_end,
    potential_now,
    potential_next,
    projector_tiles,
    tile_map,
    strengths,
    positions,
):
    space, band = lax.axis_index("space"), lax.axis_index("band")
    lower = (space % 2) == 0
    column = jnp.asarray(columns())
    plane_shape = (ROWS, LANES)
    fields_shape = (2, 4) + plane_shape
    rows_shape = (PRJ,) + plane_shape
    flags = jnp.stack([jnp.where(lower, 0.0, 1.0), jnp.where(lower, -1.0, 1.0)]).astype(f32)
    atom = (band // PRJ_ATOM).astype(jnp.int32).reshape(1)
    odd = (band % 2).astype(jnp.int32).reshape(1)

    payload = call(
        mask_kernel,
        rows_shape,
        [atom, projector_tiles.reshape(plane_shape), tile_map.reshape(4, ROWS)],
        scalars=1,
    )
    basis_own = lax.all_to_all(payload, "band", 0, 0, tiled=True)

    kept, given, own = call(
        give_kernel,
        [(4,) + plane_shape, (6,) + plane_shape, (2,) + plane_shape],
        [
            flags,
            psi_start.reshape((4,) + plane_shape),
            adjoint_end.reshape((4,) + plane_shape),
            potential_now.reshape(plane_shape),
            potential_next.reshape(plane_shape),
        ],
        scalars=1,
    )
    other = swap_core(given)
    near_message, far_message, center = call(
        pack_kernel,
        [(10,) + plane_shape, (10,) + plane_shape, fields_shape],
        [kept, own, other],
    )

    from_near = [(i, (i + 2) % 16 if i % 2 == 0 else (i - 2) % 16) for i in range(16)]
    from_far = [(j, i) for i, j in from_near]
    beside = [(i, (i + 1) % 16 if i % 2 else (i - 1) % 16) for i in range(16)]

    def exchange(fields):
        flat = fields.reshape((8,) + plane_shape)
        return (lax.ppermute(flat, "space", from_near), lax.ppermute(flat, "space", from_far))

    near = lax.ppermute(near_message, "space", from_near)
    far = lax.ppermute(far_message, "space", from_far)

    basis_own, near, far, strengths, positions = fence(
        basis_own, near, far, strengths, positions
    )
    basis_near = lax.ppermute(basis_own, "space", beside)
    basis_other = swap_core(basis_own)

    field_scratch = pltpu.VMEM(fields_shape, f32)
    work_scratch = pltpu.VMEM((4, 3) + plane_shape, f32)
    first, second, early, late = call(
        start_kernel,
        [fields_shape, fields_shape, (4,) + plane_shape, (4,) + plane_shape],
        [flags, near, far, center, own, other, column],
        scratch=[field_scratch, work_scratch],
        scalars=1,
    )
    flat_shape = (PRJ * ROWS, LANES)
    fields_flat = (8 * ROWS, LANES)
    known, ahead_flat = call(
        early_moments_kernel,
        [(16, LANES), jax.ShapeDtypeStruct((32, ROWS * LANES), jnp.bfloat16)],
        [x.reshape(fields_flat) for x in (center, first, second)]
        + [x.reshape(flat_shape) for x in (basis_own, basis_other)],
        scratch=[
            pltpu.VMEM((64, ROWS * LANES), jnp.bfloat16),
            pltpu.VMEM((128, ROWS * LANES), jnp.bfloat16),
        ],
        mib=12,
    )
    basis_near, first, second, early, late, known = fence(
        basis_near, first, second, early, late, known
    )
    kinetic_own = call(
        kinetic_kernel,
        rows_shape,
        [basis_own, basis_other, basis_near, column],
        scratch=[work_scratch],
    )
    kinetic_other = swap_core(kinetic_own)
    gram_part = call(
        gram_kernel,
        (PRJ, LANES),
        [basis_own.reshape(flat_shape), kinetic_own.reshape(flat_shape), early, late],
        scratch=[pltpu.VMEM((128, ROWS * LANES), jnp.bfloat16)],
        mib=12,
    )
    kinetic_other, gram_part = fence(kinetic_other, gram_part)
    basis = [basis_own, basis_other, kinetic_own, kinetic_other]
    part = call(
        moments_kernel,
        (16, 16, LANES),
        [known, ahead_flat] + [x.reshape(flat_shape) for x in basis] + [early, gram_part],
        scratch=[pltpu.VMEM((64, ROWS * LANES), jnp.bfloat16)],
        mib=12,
    )

    table_scratch = pltpu.VMEM((PRJ, 2, 4, 8, LANES), f32)
    rest_shape = (2, 8, LANES)
    received = lax.all_to_all(part, "space", 0, 0, tiled=True)
    received, strengths, positions, space, first, second, early, late, center = fence(
        received, strengths, positions, space, first, second, early, late, center
    )
    plane = space + jnp.stack([jnp.int32(0), 1 - 2 * (space % 2)])
    flat = np.arange(ROWS * LANES, dtype=np.int32)
    wave_x = jnp.sin(
        2.0 * math.pi / 16 * (plane[:, None] - positions[0][None, :]).astype(f32)
    )
    wave_x = jnp.broadcast_to(wave_x[:, :, None, None], (2, 4, 8, LANES))
    wave_y = jnp.sin(
        2.0 * math.pi / NY * (jnp.asarray(flat // NZ)[None, :] - positions[1][:, None]).astype(f32)
    ).reshape((4,) + plane_shape)
    wave_z = jnp.sin(
        2.0 * math.pi / NZ * (jnp.asarray(flat % NZ)[None, :] - positions[2][:, None]).astype(f32)
    ).reshape((4,) + plane_shape)
    weight = jnp.pad(strengths, (0, LANES - PRJ)).reshape(1, LANES)
    u2, rest, gram = call(
        functools.partial(advance_kernel, False),
        [fields_shape, rest_shape, (PRJ, LANES)],
        [flags, received, weight, second] + basis + [early],
        scratch=[table_scratch],
        scalars=1,
    )

    def finish(center, first, second, around, u2, rest, parts=None):
        flat = u2.reshape((8,) + plane_shape)
        near = lax.ppermute(flat, "space", from_near)
        shared = None
        if parts is not None:
            flat, parts = fence(flat, parts)
            far = lax.ppermute(flat, "space", from_far)
            shared = lax.all_to_all(parts, "band", 0, 0, tiled=True)
            rest, shared = fence(rest, shared)
        partial = call(
            partial_kernel,
            fields_shape,
            [flags, center, first, second] + basis + [around, rest],
            scratch=[table_scratch],
            scalars=1,
        )
        if parts is None:
            flat, partial = fence(flat, partial)
            far = lax.ppermute(flat, "space", from_far)
        return shared, call(
            last_kernel,
            fields_shape,
            [flags, near, far, u2, around, column, partial],
            scratch=[field_scratch] * 3 + [work_scratch],
            scalars=1,
        )

    _, mid = finish(center, first, second, early, u2, rest)
    near, far = exchange(mid)
    yours = swap_core(mid[1])
    known, basis_flat = call(
        middle_moments_kernel,
        [(24, LANES), jax.ShapeDtypeStruct((128, ROWS * LANES), jnp.bfloat16)],
        [mid, late] + basis + [wave_x, wave_y, wave_z],
    )
    first, second, part = call(
        second_kernel,
        [fields_shape, fields_shape, (16, 8, LANES)],
        [near, far, mid, late, column, basis_flat, known],
        scratch=[
            field_scratch,
            work_scratch,
            pltpu.VMEM((64, ROWS * LANES), jnp.bfloat16),
        ],
    )
    part, yours = fence(part, yours)
    received = lax.all_to_all(part, "space", 0, 0, tiled=True)
    received, first, second, late, mid, yours = fence(received, first, second, late, mid, yours)
    u2, rest = call(
        functools.partial(advance_kernel, True),
        [fields_shape, rest_shape],
        [flags, received, weight, second] + basis + [late, gram],
        scratch=[table_scratch],
        scalars=1,
    )

    u2, yours = fence(u2, yours)
    parts = call(
        payload_kernel, (16, 8, LANES), [flags, mid, yours, received, weight], scalars=1
    )
    shared, end = finish(mid, first, second, late, u2, rest, parts)
    density, forces = call(outcome_kernel, [(1, 576), (3, 4)], [odd, shared], scalars=1)

    swapped = swap_core(end[1])
    psi_end = jnp.where(lower, end[0], swapped).reshape(psi_start.shape)
    adjoint_start = jnp.where(lower, swapped, end[0]).reshape(adjoint_end.shape)
    return (psi_end, adjoint_start, density, forces)


def solution(mesh):
    return jax.shard_map(
        body,
        mesh=mesh,
        in_specs=(
            P(None, "band", "space", None),
            P(None, "band", "space", None),
            P("space", None),
            P("space", None),
            P("band", "space", None),
            P(None, "space", None),
            P(),
            P(),
        ),
        out_specs=(
            P(None, "band", "space", None),
            P(None, "band", "space", None),
            P("space", "band"),
            P(),
        ),
        check_vma=False,
    )
```

```python
import functools
import math

import jax
import jax.numpy as jnp
import numpy as np
from jax import lax
from jax.experimental import pallas as pl
from jax.experimental.pallas import tpu as pltpu
from jax.sharding import PartitionSpec as P

NB = 32
NY = 96
NZ = 96
ROWS = 72
LANES = 128
PRJ = 16
PRJ_ATOM = 4

half_step = 0.025
kinetic_scale = 3.125
highest = lax.Precision.HIGHEST
f32 = jnp.float32

A2 = -(half_step**2) / 2.0
A3 = -(half_step**3) / 6.0
A4 = half_step**4 / 24.0


def columns():
    return (np.arange(ROWS * LANES, dtype=np.int32) % NZ).reshape(ROWS, LANES)


TILES = [slice(8 * t, 8 * t + 8) for t in range(ROWS // 8)]


def next_rows(ref, index, t, x, sub):
    if t < len(TILES) - 1:
        return ref[index + (slice(8 * t + 1, 8 * t + 9),)]
    wrapped = jnp.broadcast_to(ref[index + (slice(0, 1),)], (8, LANES))
    return jnp.where(sub == 7, wrapped, pltpu.roll(x, 7, 0))


def previous_rows(ref, index, t, x, sub):
    if t > 0:
        return ref[index + (slice(8 * t - 1, 8 * t + 7),)]
    wrapped = jnp.broadcast_to(ref[index + (slice(ROWS - 1, ROWS),)], (8, LANES))
    return jnp.where(sub == 0, wrapped, pltpu.roll(x, 1, 0))


def around_plane(ref, index, column, store, scratch):
    lane = lax.broadcasted_iota(jnp.int32, (8, LANES), 1)
    sub = lax.broadcasted_iota(jnp.int32, (8, LANES), 0)
    for t, rows in enumerate(TILES):
        x = ref[index + (rows,)]
        after, before = next_rows(ref, index, t, x, sub), previous_rows(ref, index, t, x, sub)
        up = pltpu.roll(jnp.where(lane >= 96, x, after), 32, 1)
        down = pltpu.roll(jnp.where(lane < 32, x, before), 96, 1)
        place = column[rows]
        scratch[0, rows] = up + down
        scratch[1, rows] = jnp.where(place == 0, down, x)
        scratch[2, rows] = jnp.where(place == NZ - 1, up, x)
    for t, rows in enumerate(TILES):
        ahead, behind = scratch[1, rows], scratch[2, rows]
        after = next_rows(scratch, (1,), t, ahead, sub)
        before = previous_rows(scratch, (2,), t, behind, sub)
        up = pltpu.roll(jnp.where(lane >= 1, ahead, after), 127, 1)
        down = pltpu.roll(jnp.where(lane < 127, behind, before), 1, 1)
        store(rows, scratch[0, rows] + (up + down))


def fold(x):
    return jnp.sum(x.reshape(ROWS // 8, 8, LANES), axis=0)


def rows8(parts):
    sub = lax.broadcasted_iota(jnp.int32, (8, LANES), 0)
    low = sub < 4
    parts = [
        jnp.where(low, a, b) + pltpu.roll(jnp.where(low, b, a), 4, 0)
        for a, b in zip(parts[:4], parts[4:])
    ]
    for step in (2, 1):
        first = (sub & step) == 0
        parts = [
            jnp.where(first, a + pltpu.roll(a, 8 - step, 0), b + pltpu.roll(b, step, 0))
            for a, b in zip(parts[:step], parts[step:])
        ]
    return parts[0]


def params(mib):
    return pltpu.CompilerParams(vmem_limit_bytes=mib * 2**20)


VMEM = pl.BlockSpec(memory_space=pltpu.VMEM)
SMEM = pl.BlockSpec(memory_space=pltpu.SMEM)


def call(kernel, outs, args, scratch=(), scalars=0, mib=8, cost=None):
    specs = [SMEM] * scalars + [VMEM] * (len(args) - scalars)
    single = not isinstance(outs, list)
    shapes = [
        o if hasattr(o, "dtype") else jax.ShapeDtypeStruct(o, f32)
        for o in ([outs] if single else outs)
    ]
    result = pl.pallas_call(
        kernel,
        out_shape=shapes,
        in_specs=specs,
        out_specs=[VMEM] * len(shapes),
        scratch_shapes=list(scratch),
        compiler_params=params(mib),
        cost_estimate=cost,
    )(*args)
    return result[0] if single else result


def mask_kernel(atom, values_hbm, tile_map_hbm, out, values, tile_map, sems):
    copies = [
        pltpu.make_async_copy(source, target, sems.at[k])
        for k, (source, target) in enumerate([(values_hbm, values), (tile_map_hbm, tile_map)])
    ]
    for copy in copies:
        copy.start()
    for copy in copies:
        copy.wait()
    reach = tile_map[pl.ds(atom[0], 1)].astype(f32)
    row = lax.broadcasted_iota(jnp.int32, (ROWS, ROWS), 0)
    lane = lax.broadcasted_iota(jnp.int32, (ROWS, ROWS), 1)
    wide = jnp.where(row == lane, jnp.broadcast_to(reach, (ROWS, ROWS)), 0.0)
    share(out, values[...] * jnp.sum(wide, axis=1, keepdims=True))


def give_kernel(flags, psi, adjoint, now, later, kept, message, own):
    lower = flags[0] < 0.5
    for q in range(4):
        a, b = psi[q], adjoint[q]
        kept[q] = jnp.where(lower, a, b)
        message[q] = jnp.where(lower, b, a)
    own[0] = now[...]
    own[1] = later[...]
    message[4] = now[...]
    message[5] = later[...]


def pack_kernel(kept, own, other, near, far, center):
    center[0] = kept[...]
    center[1] = other[0:4]
    near[0:4] = kept[...]
    near[4:10] = other[...]
    far[0:4] = kept[...]
    far[4:8] = other[0:4]
    far[8:10] = own[...]


def kinetic_kernel(basis, basis_other, basis_near, column, out, work):
    def projector(pair, carry):
        for k in range(2):
            j = 2 * pair + k

            def store(rows, around):
                beside = basis_other[j, rows] + basis_near[j, rows]
                out[j, rows] = kinetic_scale * (6.0 * basis[j, rows] - around - beside)

            around_plane(basis, (j,), column, store, work.at[k])
        return carry

    lax.fori_loop(0, PRJ // 2, projector, 0)


def two_steps(near, far, center, potential, column, first, mixed, second, work):
    def row(q, carry):
        sides = [(0, 1, near, 4 + q, q), (1, 0, far, q, 4 + q)]
        for plane, across, message, edge, beyond in sides:

            def store(r, around, plane=plane, across=across, message=message, edge=edge):
                x, e = center[plane, q, r], message[edge, r]
                value = kinetic_scale * (6.0 * x - around - (e + center[across, q, r]))
                value = value + potential[plane, r] * x
                first[plane, q, r] = value
                mixed[plane, q, r] = value - kinetic_scale * e

            around_plane(center, (plane, q), column, store, work.at[plane])
        for plane, across, message, edge, beyond in sides:

            def store(r, around, plane=plane, across=across, message=message, edge=edge, beyond=beyond):
                f, e = first[plane, q, r], message[edge, r]
                beside = kinetic_scale * (6.0 * e - message[beyond, r] - center[plane, q, r])
                beside = beside + potential[2 + plane, r] * e + first[across, q, r]
                value = kinetic_scale * (6.0 * f - around - beside)
                second[plane, q, r] = value + potential[plane, r] * f

            around_plane(mixed, (plane, q), column, store, work.at[2 + plane])
        return carry

    lax.fori_loop(0, 4, row, 0)


def spread(parts, lanes):
    total = jnp.concatenate([rows8(parts[k : k + 8]) for k in range(0, len(parts), 8)], 0)
    summed = jnp.sum(total, axis=1, keepdims=True)
    lane = lax.broadcasted_iota(jnp.int32, total.shape, 1)
    return jnp.where(lane == lanes, summed, 0.0)


def start_kernel(flags, near, far, center, own, other, column, first, second, early, late, edge, work):
    lower = flags[0] < 0.5
    pairs = [(own.at[0], own.at[1]), (other.at[4], other.at[5])]
    pairs += [(near.at[8], near.at[9]), (far.at[8], far.at[9])]
    for k, (a, b) in enumerate(pairs):
        a, b = a[...], b[...]
        early[k] = jnp.where(lower, a, b)
        late[k] = jnp.where(lower, b, a)
    two_steps(near, far, center, early, column, first, edge, second, work)


def project(basis, potential, kinds, count):
    def projector(j, total):
        parts = [[None] * 4 for _ in kinds]
        for plane in range(2):
            beta = basis[plane][j]
            wide = None if len(basis) == 2 else basis[2 + plane][j] + potential[plane] * beta
            for k, (field, by) in enumerate(kinds):
                factor = wide if by == "wide" else beta if by is None else by(plane, j, beta)
                for q in range(4):
                    value = fold(field[plane, q] * factor)
                    parts[k][q] = value if plane == 0 else parts[k][q] + value
        flat = [value for part in parts for value in part]
        flat += [jnp.zeros((8, LANES), f32)] * (count - len(flat))
        return total + spread(flat, j)

    return lax.fori_loop(0, PRJ, projector, jnp.zeros((count, LANES), f32))


def share(out, value):
    def copy(k, carry):
        out[k] = value
        return carry

    lax.fori_loop(0, 16, copy, 0)


def split(x):
    high = x.astype(jnp.bfloat16)
    return high, (x - high.astype(f32)).astype(jnp.bfloat16)


def put(target, row, lanes, value, offset):
    high, low = split(value)
    target[row : row + PRJ, lanes] = high
    target[row + offset : row + offset + PRJ, lanes] = low


def flat_rows(ref, s, count):
    return ref[pl.ds(s, count, stride=ROWS)]


def lanes_at(s):
    return pl.ds(pl.multiple_of(s * LANES, LANES), LANES)


def products(a, b):
    return lax.dot_general(a[...], b[...], (((1,), (1,)), ((), ())), preferred_element_type=f32)


def gram_kernel(basis, kinetic, early, late, out, flat):
    def row(s, carry):
        beta, moved = flat_rows(basis, s, PRJ), flat_rows(kinetic, s, PRJ)
        at = lanes_at(s)
        put(flat, 0, at, beta, 64)
        for k, v in enumerate((early, late)):
            put(flat, PRJ * (k + 1), at, moved + v[0, pl.ds(s, 1)] * beta, 64)
        return carry

    for k in (48, 112):
        flat[k : k + PRJ] = jnp.zeros((PRJ, ROWS * LANES), jnp.bfloat16)
    lax.fori_loop(0, ROWS, row, 0, unroll=8)
    both = products(flat, flat)
    both = both[:64] + both[64:]
    both = both + pltpu.roll(both, 64, 1)
    lane = lax.broadcasted_iota(jnp.int32, (PRJ, LANES), 1)
    out[...] = (
        jnp.where((lane >= 16) & (lane < 64), pltpu.roll(both[:16], 16, 1), 0.0)
        + jnp.where((lane >= 64) & (lane < 80), pltpu.roll(both[16:32], 48, 1), 0.0)
        + jnp.where((lane >= 80) & (lane < 96), pltpu.roll(both[32:48], 48, 1), 0.0)
    )


def put_fields(fields, flat):
    def row(s, carry):
        at = lanes_at(s)
        values = [flat_rows(field, s, 8) for field in fields]
        for k in range(0, len(values), 2):
            pair = values[k : k + 2]
            pair = pair if len(pair) == 2 else pair * 2
            put(flat, 8 * k, at, jnp.concatenate(pair, 0), 32)
        return carry

    lax.fori_loop(0, ROWS, row, 0, unroll=8)


def put_basis(own, other, own_k, other_k, potential, flat):
    def row(s, carry):
        at = lanes_at(s)
        for plane, (b, k) in enumerate(((own, own_k), (other, other_k))):
            beta, moved = flat_rows(b, s, PRJ), flat_rows(k, s, PRJ)
            put(flat, 2 * PRJ * plane, at, beta, 64)
            put(flat, 2 * PRJ * plane + PRJ, at, moved + potential[plane, pl.ds(s, 1)] * beta, 64)
        return carry

    lax.fori_loop(0, ROWS, row, 0, unroll=8)


def field_moments(fields_flat, basis_flat, count):
    both = products(fields_flat, basis_flat)
    both = both[:32] + both[32:]
    both = both + pltpu.roll(both, 64, 1)
    result = []
    for k in range(count):
        part = both[8 * k : 8 * k + 8]
        result.append(part + pltpu.roll(pltpu.roll(part, 96, 1), 4, 0))
    return result


def stack_rows(a, b):
    sub = lax.broadcasted_iota(jnp.int32, (8, LANES), 0)
    lane = lax.broadcasted_iota(jnp.int32, (8, LANES), 1)
    return jnp.where(lane < PRJ, jnp.where(sub < 4, a, pltpu.roll(b, 4, 0)), 0.0)


def early_moments_kernel(center, first, second, own, other, out, ahead_flat, fields_flat, basis_flat):
    put_fields((center, first, second), fields_flat)

    def row(s, carry):
        at = lanes_at(s)
        for plane, b in enumerate((own, other)):
            put(basis_flat, 2 * PRJ * plane, at, flat_rows(b, s, PRJ), 64)
        return carry

    for k in (16, 48, 80, 112):
        basis_flat[k : k + PRJ] = jnp.zeros((PRJ, ROWS * LANES), jnp.bfloat16)
    lax.fori_loop(0, ROWS, row, 0, unroll=8)
    found = field_moments(fields_flat, basis_flat, 3)
    out[...] = jnp.concatenate([stack_rows(found[0], found[1]), stack_rows(found[2], 0.0 * found[2])], 0)
    ahead_flat[0:16] = fields_flat[16:32]
    ahead_flat[16:32] = fields_flat[48:64]


def moments_kernel(known, ahead_flat, own, other, own_k, other_k, potential, gram, out, basis_flat):
    def row(s, carry):
        at = lanes_at(s)
        for plane, (b, k) in enumerate(((own, own_k), (other, other_k))):
            wide = flat_rows(k, s, PRJ) + potential[plane, pl.ds(s, 1)] * flat_rows(b, s, PRJ)
            put(basis_flat, PRJ * plane, at, wide, 32)
        return carry

    lax.fori_loop(0, ROWS, row, 0, unroll=8)
    both = products(ahead_flat, basis_flat)
    both = both[:8] + both[16:24]
    both = both[:, :32] + both[:, 32:]
    both = jnp.concatenate([both, jnp.zeros((8, LANES - 32), f32)], 1)
    wide = both + pltpu.roll(pltpu.roll(both, LANES - PRJ, 1), 4, 0)
    moments = jnp.concatenate([known[...][:8], known[...][8:] + stack_rows(0.0 * wide, wide)], 0)
    share(out, moments + gram[...])


def middle_moments_kernel(
    center, potential, own, other, own_k, other_k, wave_x, wave_y, wave_z, out, basis_flat
):
    kinds = [
        (center, None),
        (center, "wide"),
        (center, lambda plane, j, beta: beta * wave_x[plane, j // PRJ_ATOM, 0:1]),
        (center, lambda plane, j, beta: beta * wave_y[j // PRJ_ATOM]),
        (center, lambda plane, j, beta: beta * wave_z[j // PRJ_ATOM]),
    ]
    out[...] = project((own, other, own_k, other_k), potential, kinds, 24)
    flat = [x.reshape(PRJ * ROWS, LANES) for x in (own, other, own_k, other_k)]
    put_basis(*flat, potential, basis_flat)


def second_kernel(
    near, far, center, potential, column, basis_flat, known, first, second, out, edge, work, fields_flat
):
    two_steps(near, far, center, potential, column, first, edge, second, work)
    put_fields([x.reshape(8 * ROWS, LANES) for x in (first, second)], fields_flat)
    found = [pltpu.roll(x, LANES - PRJ, 1) for x in field_moments(fields_flat, basis_flat, 2)]
    value = known[...]
    packed = value[:8] + pltpu.roll(stack_rows(*found), PRJ, 1)
    packed = packed + pltpu.roll(value[8:16], 2 * PRJ, 1) + pltpu.roll(value[16:], 3 * PRJ, 1)
    share(out, packed)


def times_i(x):
    row = lax.broadcasted_iota(jnp.int32, (8, LANES), 0)
    return jnp.where(row < 2, -pltpu.roll(x, 6, 0), pltpu.roll(x, 2, 0))


def coefficients(later, flags, received, strengths, gram):
    upper, sign = flags[0], flags[1]
    sums = []
    for core in range(2):
        acc = received[core]
        for k in range(core + 2, 16, 2):
            acc = acc + received[k]
        sums.append(acc)
    mine = jnp.where(upper > 0.5, sums[1], sums[0])
    if later:
        mine = jnp.concatenate([mine, pltpu.roll(mine, LANES - PRJ, 1)], 0)
    lane = lax.broadcasted_iota(jnp.int32, (PRJ, LANES), 1)
    valid = lane < PRJ
    if later:
        grams = gram[...]
    else:
        theirs = jnp.where(upper > 0.5, sums[0], sums[1])
        turned = jnp.where(
            (lane >= 48) & (lane < 64) | (lane >= 80),
            pltpu.roll(theirs, PRJ, 1),
            pltpu.roll(theirs, LANES - PRJ, 1),
        )
        grams = mine + jnp.where(lane < 32, theirs, turned)
        gram[...] = grams

    def block(k):
        return jnp.where(valid, pltpu.roll(grams, LANES - PRJ * (k + 1), 1), 0.0)

    g0 = block(0)
    g1, g2 = (block(2), block(4)) if later else (block(1), block(3))
    weight = strengths[...]

    def moment(k):
        rolled = mine if k == 0 else pltpu.roll(mine, PRJ - 4 * k, 0)
        return jnp.where(valid, rolled, 0.0)[:8]

    def apply(c, g):
        return jnp.dot(c[:, :PRJ], g, precision=highest, preferred_element_type=f32)

    c0 = weight * moment(0)
    c1 = weight * (moment(1) + apply(c0, g0))
    c2 = weight * (moment(2) + apply(c0, g1) + apply(c1, g0))
    c3 = weight * (moment(3) + apply(c0, g2) + apply(c1, g1) + apply(c2, g0))
    e0 = times_i((sign * half_step) * c0 + (sign * A3) * c2) + A2 * c1 + A4 * c3
    e1 = A2 * c0 + A4 * c2
    return c0, c1, e0, e1


def spread_table(table, sets):
    row = lax.broadcasted_iota(jnp.int32, (PRJ, LANES), 0)
    lane = lax.broadcasted_iota(jnp.int32, (PRJ, LANES), 1)
    for k, c in enumerate(sets):
        for q in range(4):
            wide = jnp.broadcast_to(c[q : q + 1], (PRJ, LANES))
            column = jnp.sum(jnp.where(row == lane, wide, 0.0), axis=1, keepdims=True)
            for j in range(PRJ):
                table[j, k, q] = jnp.broadcast_to(column[j : j + 1], (8, LANES))


def combine(out, start, basis, potential, table):
    def tile(i, carry):
        rows = pl.ds(pl.multiple_of(i * 8, 8), 8)
        totals = [start(plane, rows) for plane in range(2)]
        v = [potential[plane, rows] for plane in range(2)]
        for j in range(PRJ):
            by_wide = [table[j, 0, q] for q in range(4)]
            by_beta = [table[j, 1, q] for q in range(4)]
            for plane, total in enumerate(totals):
                beta = basis[plane][j, rows]
                wide = basis[2 + plane][j, rows] + v[plane] * beta
                for q in range(4):
                    total[q] = total[q] + by_wide[q] * wide + by_beta[q] * beta
        for plane, total in enumerate(totals):
            for q in range(4):
                out[plane, q, rows] = total[q]
        return carry

    lax.fori_loop(0, ROWS // 8, tile, 0)


def advance_kernel(later, flags, received, strengths, second, own, other, own_k, other_k, potential, *refs):
    if later:
        gram, out, rest, table = refs
    else:
        out, rest, gram, table = refs
    c0, c1, e0, e1 = coefficients(later, flags, received, strengths, gram)
    rest[0] = e1
    rest[1] = e0
    spread_table(table, (c0, c1))

    def start(plane, rows):
        return [second[plane, q, rows] for q in range(4)]

    combine(out, start, (own, other, own_k, other_k), potential, table)


def partial_kernel(flags, center, first, second, own, other, own_k, other_k, potential, rest, out, table):
    sign = flags[1]
    spread_table(table, (rest[0], rest[1]))

    def start(plane, rows):
        moved = [first[plane, q, rows] for q in range(4)]
        mixed = [-moved[2], -moved[3], moved[0], moved[1]]
        return [
            center[plane, q, rows] + (sign * half_step) * mixed[q] + A2 * second[plane, q, rows]
            for q in range(4)
        ]

    combine(out, start, (own, other, own_k, other_k), potential, table)


def last_kernel(flags, near, far, center, potential, column, partial, out, first, edge, second, work):
    two_steps(near, far, center, potential, column, first, edge, second, work)
    sign = flags[1]
    for plane in range(2):
        for q in range(4):
            mixed = -first[plane, q + 2] if q < 2 else first[plane, q - 2]
            out[plane, q] = partial[plane, q] + (sign * A3) * mixed + A4 * second[plane, q]


def payload_kernel(flags, mine, yours, received, strengths, out):
    turned = [mine[0, q] * yours[q + 2] - mine[0, q + 2] * yours[q] for q in range(2)]
    density = (-2.0 * half_step * flags[1]) * (turned[0] + turned[1])
    sums = []
    for core in range(2):
        acc = received[core]
        for k in range(core + 2, 16, 2):
            acc = acc + received[k]
        sums.append(acc)
    forces = []
    for q in range(3):
        rows, shift = slice(4 * (q % 2), 4 * (q % 2) + 4), LANES - (2 + q // 2) * PRJ
        slopes = [pltpu.roll(x, shift, 1)[rows] for x in sums]
        products = sums[0][:4] * slopes[1] + sums[1][:4] * slopes[0]
        forces.append(strengths[...] * jnp.sum(products, axis=0, keepdims=True))
    for k in range(16):
        first = 9 * k // 2
        out[k] = jnp.concatenate([density[first : first + 5]] + forces, 0)


def outcome_kernel(odd, received, density, forces):
    total = received[0]
    for k in range(1, 16):
        total = total + received[k]
    lane = lax.broadcasted_iota(jnp.int32, (1, LANES), 1)
    moved = pltpu.roll(total, 64, 1)
    for k in range(5):
        start = total[k : k + 1]
        shifted = jnp.where(lane < 64, moved[k : k + 1], moved[min(k + 1, 4) : min(k + 1, 4) + 1])
        row = jnp.where(odd[0] > 0, shifted, start)
        width = min(LANES, 576 - k * LANES)
        density[:, k * LANES : k * LANES + width] = row[:, :width]
    atom = lax.broadcasted_iota(jnp.int32, (3, LANES), 1) // PRJ_ATOM
    column = lax.broadcasted_iota(jnp.int32, (3, 4), 1)
    result = jnp.zeros((3, 4), f32)
    for a in range(4):
        part = jnp.sum(jnp.where(atom == a, total[5:8], 0.0), axis=1, keepdims=True)
        result = jnp.where(column == a, part * (1.0 / NB), result)
    forces[...] = result


def swap_core(x):
    return lax.ppermute(x, "space", [(i, i ^ 1) for i in range(16)])


def fence(*values):
    return lax.optimization_barrier(values)


def body(
    psi_start,
    adjoint_end,
    potential_now,
    potential_next,
    projector_tiles,
    tile_map,
    strengths,
    positions,
):
    space, band = lax.axis_index("space"), lax.axis_index("band")
    lower = (space % 2) == 0
    column = jnp.asarray(columns())
    plane_shape = (ROWS, LANES)
    fields_shape = (2, 4) + plane_shape
    rows_shape = (PRJ,) + plane_shape
    flags = jnp.stack([jnp.where(lower, 0.0, 1.0), jnp.where(lower, -1.0, 1.0)]).astype(f32)
    atom = (band // PRJ_ATOM).astype(jnp.int32).reshape(1)
    odd = (band % 2).astype(jnp.int32).reshape(1)

    far_memory = pl.BlockSpec(memory_space=pltpu.HBM)
    payload = pl.pallas_call(
        mask_kernel,
        out_shape=jax.ShapeDtypeStruct(rows_shape, f32),
        in_specs=[SMEM, far_memory, far_memory],
        out_specs=VMEM,
        scratch_shapes=[
            pltpu.VMEM(plane_shape, f32),
            pltpu.VMEM((4, ROWS), jnp.int32),
            pltpu.SemaphoreType.DMA((2,)),
        ],
        compiler_params=params(60),
    )(atom, projector_tiles.reshape(plane_shape), tile_map.reshape(4, ROWS))
    basis_own = lax.all_to_all(payload, "band", 0, 0, tiled=True)

    kept, given, own = call(
        give_kernel,
        [(4,) + plane_shape, (6,) + plane_shape, (2,) + plane_shape],
        [
            flags,
            psi_start.reshape((4,) + plane_shape),
            adjoint_end.reshape((4,) + plane_shape),
            potential_now.reshape(plane_shape),
            potential_next.reshape(plane_shape),
        ],
        scalars=1,
    )
    other = swap_core(given)
    near_message, far_message, center = call(
        pack_kernel,
        [(10,) + plane_shape, (10,) + plane_shape, fields_shape],
        [kept, own, other],
    )

    from_near = [(i, (i + 2) % 16 if i % 2 == 0 else (i - 2) % 16) for i in range(16)]
    from_far = [(j, i) for i, j in from_near]
    beside = [(i, (i + 1) % 16 if i % 2 else (i - 1) % 16) for i in range(16)]

    def exchange(fields):
        flat = fields.reshape((8,) + plane_shape)
        return (lax.ppermute(flat, "space", from_near), lax.ppermute(flat, "space", from_far))

    near = lax.ppermute(near_message, "space", from_near)
    far = lax.ppermute(far_message, "space", from_far)

    basis_own, near, far, strengths, positions = fence(
        basis_own, near, far, strengths, positions
    )
    basis_near = lax.ppermute(basis_own, "space", beside)
    basis_other = swap_core(basis_own)

    field_scratch = pltpu.VMEM(fields_shape, f32)
    work_scratch = pltpu.VMEM((4, 3) + plane_shape, f32)
    first, second, early, late = call(
        start_kernel,
        [fields_shape, fields_shape, (4,) + plane_shape, (4,) + plane_shape],
        [flags, near, far, center, own, other, column],
        scratch=[field_scratch, work_scratch],
        scalars=1,
    )
    flat_shape = (PRJ * ROWS, LANES)
    fields_flat = (8 * ROWS, LANES)
    known, ahead_flat = call(
        early_moments_kernel,
        [(16, LANES), jax.ShapeDtypeStruct((32, ROWS * LANES), jnp.bfloat16)],
        [x.reshape(fields_flat) for x in (center, first, second)]
        + [x.reshape(flat_shape) for x in (basis_own, basis_other)],
        scratch=[
            pltpu.VMEM((64, ROWS * LANES), jnp.bfloat16),
            pltpu.VMEM((128, ROWS * LANES), jnp.bfloat16),
        ],
        mib=12,
    )
    basis_near, first, second, early, late, known = fence(
        basis_near, first, second, early, late, known
    )
    kinetic_own = call(
        kinetic_kernel,
        rows_shape,
        [basis_own, basis_other, basis_near, column],
        scratch=[work_scratch],
    )
    kinetic_other = swap_core(kinetic_own)
    gram_part = call(
        gram_kernel,
        (PRJ, LANES),
        [basis_own.reshape(flat_shape), kinetic_own.reshape(flat_shape), early, late],
        scratch=[pltpu.VMEM((128, ROWS * LANES), jnp.bfloat16)],
        mib=12,
    )
    kinetic_other, gram_part = fence(kinetic_other, gram_part)
    basis = [basis_own, basis_other, kinetic_own, kinetic_other]
    part = call(
        moments_kernel,
        (16, 16, LANES),
        [known, ahead_flat] + [x.reshape(flat_shape) for x in basis] + [early, gram_part],
        scratch=[pltpu.VMEM((64, ROWS * LANES), jnp.bfloat16)],
        mib=12,
    )

    table_scratch = pltpu.VMEM((PRJ, 2, 4, 8, LANES), f32)
    rest_shape = (2, 8, LANES)
    received = lax.all_to_all(part, "space", 0, 0, tiled=True)
    received, strengths, positions, space, first, second, early, late, center = fence(
        received, strengths, positions, space, first, second, early, late, center
    )
    plane = space + jnp.stack([jnp.int32(0), 1 - 2 * (space % 2)])
    flat = np.arange(ROWS * LANES, dtype=np.int32)
    wave_x = jnp.sin(
        2.0 * math.pi / 16 * (plane[:, None] - positions[0][None, :]).astype(f32)
    )
    wave_x = jnp.broadcast_to(wave_x[:, :, None, None], (2, 4, 8, LANES))
    wave_y = jnp.sin(
        2.0 * math.pi / NY * (jnp.asarray(flat // NZ)[None, :] - positions[1][:, None]).astype(f32)
    ).reshape((4,) + plane_shape)
    wave_z = jnp.sin(
        2.0 * math.pi / NZ * (jnp.asarray(flat % NZ)[None, :] - positions[2][:, None]).astype(f32)
    ).reshape((4,) + plane_shape)
    weight = jnp.pad(strengths, (0, LANES - PRJ)).reshape(1, LANES)
    u2, rest, gram = call(
        functools.partial(advance_kernel, False),
        [fields_shape, rest_shape, (PRJ, LANES)],
        [flags, received, weight, second] + basis + [early],
        scratch=[table_scratch],
        scalars=1,
    )

    def finish(center, first, second, around, u2, rest, parts=None):
        flat = u2.reshape((8,) + plane_shape)
        near = lax.ppermute(flat, "space", from_near)
        shared = None
        if parts is not None:
            flat, parts = fence(flat, parts)
            far = lax.ppermute(flat, "space", from_far)
            shared = lax.all_to_all(parts, "band", 0, 0, tiled=True)
            rest, shared = fence(rest, shared)
        partial = call(
            partial_kernel,
            fields_shape,
            [flags, center, first, second] + basis + [around, rest],
            scratch=[table_scratch],
            scalars=1,
        )
        if parts is None:
            flat, partial = fence(flat, partial)
            far = lax.ppermute(flat, "space", from_far)
        return shared, call(
            last_kernel,
            fields_shape,
            [flags, near, far, u2, around, column, partial],
            scratch=[field_scratch] * 3 + [work_scratch],
            scalars=1,
        )

    _, mid = finish(center, first, second, early, u2, rest)
    near, far = exchange(mid)
    yours = swap_core(mid[1])
    known, basis_flat = call(
        middle_moments_kernel,
        [(24, LANES), jax.ShapeDtypeStruct((128, ROWS * LANES), jnp.bfloat16)],
        [mid, late] + basis + [wave_x, wave_y, wave_z],
    )
    first, second, part = call(
        second_kernel,
        [fields_shape, fields_shape, (16, 8, LANES)],
        [near, far, mid, late, column, basis_flat, known],
        scratch=[
            field_scratch,
            work_scratch,
            pltpu.VMEM((64, ROWS * LANES), jnp.bfloat16),
        ],
    )
    part, yours = fence(part, yours)
    received = lax.all_to_all(part, "space", 0, 0, tiled=True)
    received, first, second, late, mid, yours = fence(received, first, second, late, mid, yours)
    u2, rest = call(
        functools.partial(advance_kernel, True),
        [fields_shape, rest_shape],
        [flags, received, weight, second] + basis + [late, gram],
        scratch=[table_scratch],
        scalars=1,
    )

    u2, yours = fence(u2, yours)
    parts = call(
        payload_kernel, (16, 8, LANES), [flags, mid, yours, received, weight], scalars=1
    )
    shared, end = finish(mid, first, second, late, u2, rest, parts)
    density, forces = call(outcome_kernel, [(1, 576), (3, 4)], [odd, shared], scalars=1)

    swapped = swap_core(end[1])
    psi_end = jnp.where(lower, end[0], swapped).reshape(psi_start.shape)
    adjoint_start = jnp.where(lower, swapped, end[0]).reshape(adjoint_end.shape)
    return (psi_end, adjoint_start, density, forces)


def solution(mesh):
    return jax.shard_map(
        body,
        mesh=mesh,
        in_specs=(
            P(None, "band", "space", None),
            P(None, "band", "space", None),
            P("space", None),
            P("space", None),
            P("band", "space", None),
            P(None, "space", None),
            P(),
            P(),
        ),
        out_specs=(
            P(None, "band", "space", None),
            P(None, "band", "space", None),
            P("space", "band"),
            P(),
        ),
        check_vma=False,
    )
```

```python
import functools
import math

import jax
import jax.numpy as jnp
import numpy as np
from jax import lax
from jax.experimental import pallas as pl
from jax.experimental.pallas import tpu as pltpu
from jax.sharding import PartitionSpec as P

NB = 32
NY = 96
NZ = 96
ROWS = 72
LANES = 128
PRJ = 16
PRJ_ATOM = 4

half_step = 0.025
kinetic_scale = 3.125
highest = lax.Precision.HIGHEST
f32 = jnp.float32

A2 = -(half_step**2) / 2.0
A3 = -(half_step**3) / 6.0
A4 = half_step**4 / 24.0


def columns():
    return (np.arange(ROWS * LANES, dtype=np.int32) % NZ).reshape(ROWS, LANES)


TILES = [slice(8 * t, 8 * t + 8) for t in range(ROWS // 8)]


def next_rows(ref, index, t, x, sub):
    if t < len(TILES) - 1:
        return ref[index + (slice(8 * t + 1, 8 * t + 9),)]
    wrapped = jnp.broadcast_to(ref[index + (slice(0, 1),)], (8, LANES))
    return jnp.where(sub == 7, wrapped, pltpu.roll(x, 7, 0))


def previous_rows(ref, index, t, x, sub):
    if t > 0:
        return ref[index + (slice(8 * t - 1, 8 * t + 7),)]
    wrapped = jnp.broadcast_to(ref[index + (slice(ROWS - 1, ROWS),)], (8, LANES))
    return jnp.where(sub == 0, wrapped, pltpu.roll(x, 1, 0))


def around_plane(ref, index, column, store, scratch):
    lane = lax.broadcasted_iota(jnp.int32, (8, LANES), 1)
    sub = lax.broadcasted_iota(jnp.int32, (8, LANES), 0)
    for t, rows in enumerate(TILES):
        x = ref[index + (rows,)]
        after, before = next_rows(ref, index, t, x, sub), previous_rows(ref, index, t, x, sub)
        up = pltpu.roll(jnp.where(lane >= 96, x, after), 32, 1)
        down = pltpu.roll(jnp.where(lane < 32, x, before), 96, 1)
        place = column[rows]
        scratch[0, rows] = up + down
        scratch[1, rows] = jnp.where(place == 0, down, x)
        scratch[2, rows] = jnp.where(place == NZ - 1, up, x)
    for t, rows in enumerate(TILES):
        ahead, behind = scratch[1, rows], scratch[2, rows]
        after = next_rows(scratch, (1,), t, ahead, sub)
        before = previous_rows(scratch, (2,), t, behind, sub)
        up = pltpu.roll(jnp.where(lane >= 1, ahead, after), 127, 1)
        down = pltpu.roll(jnp.where(lane < 127, behind, before), 1, 1)
        store(rows, scratch[0, rows] + (up + down))


def fold(x):
    return jnp.sum(x.reshape(ROWS // 8, 8, LANES), axis=0)


def rows8(parts):
    sub = lax.broadcasted_iota(jnp.int32, (8, LANES), 0)
    low = sub < 4
    parts = [
        jnp.where(low, a, b) + pltpu.roll(jnp.where(low, b, a), 4, 0)
        for a, b in zip(parts[:4], parts[4:])
    ]
    for step in (2, 1):
        first = (sub & step) == 0
        parts = [
            jnp.where(first, a + pltpu.roll(a, 8 - step, 0), b + pltpu.roll(b, step, 0))
            for a, b in zip(parts[:step], parts[step:])
        ]
    return parts[0]


def params(mib):
    return pltpu.CompilerParams(vmem_limit_bytes=mib * 2**20)


VMEM = pl.BlockSpec(memory_space=pltpu.VMEM)
SMEM = pl.BlockSpec(memory_space=pltpu.SMEM)


def call(kernel, outs, args, scratch=(), scalars=0, mib=8, cost=None):
    specs = [SMEM] * scalars + [VMEM] * (len(args) - scalars)
    single = not isinstance(outs, list)
    shapes = [
        o if hasattr(o, "dtype") else jax.ShapeDtypeStruct(o, f32)
        for o in ([outs] if single else outs)
    ]
    result = pl.pallas_call(
        kernel,
        out_shape=shapes,
        in_specs=specs,
        out_specs=[VMEM] * len(shapes),
        scratch_shapes=list(scratch),
        compiler_params=params(mib),
        cost_estimate=cost,
    )(*args)
    return result[0] if single else result


def mask_kernel(atom, values_hbm, tile_map_hbm, out, values, tile_map, sems):
    copies = [
        pltpu.make_async_copy(source, target, sems.at[k])
        for k, (source, target) in enumerate([(values_hbm, values), (tile_map_hbm, tile_map)])
    ]
    for copy in copies:
        copy.start()
    for copy in copies:
        copy.wait()
    reach = tile_map[pl.ds(atom[0], 1)].astype(f32)
    row = lax.broadcasted_iota(jnp.int32, (ROWS, ROWS), 0)
    lane = lax.broadcasted_iota(jnp.int32, (ROWS, ROWS), 1)
    wide = jnp.where(row == lane, jnp.broadcast_to(reach, (ROWS, ROWS)), 0.0)
    share(out, values[...] * jnp.sum(wide, axis=1, keepdims=True))


def give_kernel(flags, psi, adjoint, now, later, kept, message, own):
    lower = flags[0] < 0.5
    for q in range(4):
        a, b = psi[q], adjoint[q]
        kept[q] = jnp.where(lower, a, b)
        message[q] = jnp.where(lower, b, a)
    own[0] = now[...]
    own[1] = later[...]
    message[4] = now[...]
    message[5] = later[...]


def pack_kernel(kept, own, other, near, far, center):
    center[0] = kept[...]
    center[1] = other[0:4]
    near[0:4] = kept[...]
    near[4:10] = other[...]
    far[0:4] = kept[...]
    far[4:8] = other[0:4]
    far[8:10] = own[...]


def kinetic_kernel(basis, basis_other, basis_near, column, out, work):
    def projector(pair, carry):
        for k in range(2):
            j = 2 * pair + k

            def store(rows, around):
                beside = basis_other[j, rows] + basis_near[j, rows]
                out[j, rows] = kinetic_scale * (6.0 * basis[j, rows] - around - beside)

            around_plane(basis, (j,), column, store, work.at[k])
        return carry

    lax.fori_loop(0, PRJ // 2, projector, 0)


def two_steps(near, far, center, potential, column, first, mixed, second, work):
    def row(q, carry):
        sides = [(0, 1, near, 4 + q, q), (1, 0, far, q, 4 + q)]
        for plane, across, message, edge, beyond in sides:

            def store(r, around, plane=plane, across=across, message=message, edge=edge):
                x, e = center[plane, q, r], message[edge, r]
                value = kinetic_scale * (6.0 * x - around - (e + center[across, q, r]))
                value = value + potential[plane, r] * x
                first[plane, q, r] = value
                mixed[plane, q, r] = value - kinetic_scale * e

            around_plane(center, (plane, q), column, store, work.at[plane])
        for plane, across, message, edge, beyond in sides:

            def store(r, around, plane=plane, across=across, message=message, edge=edge, beyond=beyond):
                f, e = first[plane, q, r], message[edge, r]
                beside = kinetic_scale * (6.0 * e - message[beyond, r] - center[plane, q, r])
                beside = beside + potential[2 + plane, r] * e + first[across, q, r]
                value = kinetic_scale * (6.0 * f - around - beside)
                second[plane, q, r] = value + potential[plane, r] * f

            around_plane(mixed, (plane, q), column, store, work.at[2 + plane])
        return carry

    lax.fori_loop(0, 4, row, 0)


def spread(parts, lanes):
    total = jnp.concatenate([rows8(parts[k : k + 8]) for k in range(0, len(parts), 8)], 0)
    summed = jnp.sum(total, axis=1, keepdims=True)
    lane = lax.broadcasted_iota(jnp.int32, total.shape, 1)
    return jnp.where(lane == lanes, summed, 0.0)


def start_kernel(flags, near, far, center, own, other, column, first, second, early, late, edge, work):
    lower = flags[0] < 0.5
    pairs = [(own.at[0], own.at[1]), (other.at[4], other.at[5])]
    pairs += [(near.at[8], near.at[9]), (far.at[8], far.at[9])]
    for k, (a, b) in enumerate(pairs):
        a, b = a[...], b[...]
        early[k] = jnp.where(lower, a, b)
        late[k] = jnp.where(lower, b, a)
    two_steps(near, far, center, early, column, first, edge, second, work)


def project(basis, potential, kinds, count):
    def projector(j, total):
        parts = [[None] * 4 for _ in kinds]
        for plane in range(2):
            beta = basis[plane][j]
            wide = None if len(basis) == 2 else basis[2 + plane][j] + potential[plane] * beta
            for k, (field, by) in enumerate(kinds):
                factor = wide if by == "wide" else beta if by is None else by(plane, j, beta)
                for q in range(4):
                    value = fold(field[plane, q] * factor)
                    parts[k][q] = value if plane == 0 else parts[k][q] + value
        flat = [value for part in parts for value in part]
        flat += [jnp.zeros((8, LANES), f32)] * (count - len(flat))
        return total + spread(flat, j)

    return lax.fori_loop(0, PRJ, projector, jnp.zeros((count, LANES), f32))


def share(out, value):
    def copy(k, carry):
        out[k] = value
        return carry

    lax.fori_loop(0, 16, copy, 0)


def split(x):
    high = x.astype(jnp.bfloat16)
    return high, (x - high.astype(f32)).astype(jnp.bfloat16)


def put(target, row, lanes, value, offset):
    high, low = split(value)
    target[row : row + PRJ, lanes] = high
    target[row + offset : row + offset + PRJ, lanes] = low


def flat_rows(ref, s, count):
    return ref[pl.ds(s, count, stride=ROWS)]


def lanes_at(s):
    return pl.ds(pl.multiple_of(s * LANES, LANES), LANES)


def products(a, b):
    return lax.dot_general(a[...], b[...], (((1,), (1,)), ((), ())), preferred_element_type=f32)


def gram_kernel(basis, kinetic, early, late, out, flat):
    def row(s, carry):
        beta, moved = flat_rows(basis, s, PRJ), flat_rows(kinetic, s, PRJ)
        at = lanes_at(s)
        put(flat, 0, at, beta, 64)
        for k, v in enumerate((early, late)):
            put(flat, PRJ * (k + 1), at, moved + v[0, pl.ds(s, 1)] * beta, 64)
        return carry

    for k in (48, 112):
        flat[k : k + PRJ] = jnp.zeros((PRJ, ROWS * LANES), jnp.bfloat16)
    lax.fori_loop(0, ROWS, row, 0, unroll=8)
    both = products(flat, flat)
    both = both[:64] + both[64:]
    both = both + pltpu.roll(both, 64, 1)
    lane = lax.broadcasted_iota(jnp.int32, (PRJ, LANES), 1)
    out[...] = (
        jnp.where((lane >= 16) & (lane < 64), pltpu.roll(both[:16], 16, 1), 0.0)
        + jnp.where((lane >= 64) & (lane < 80), pltpu.roll(both[16:32], 48, 1), 0.0)
        + jnp.where((lane >= 80) & (lane < 96), pltpu.roll(both[32:48], 48, 1), 0.0)
    )


def put_fields(fields, flat):
    def row(s, carry):
        at = lanes_at(s)
        values = [flat_rows(field, s, 8) for field in fields]
        for k in range(0, len(values), 2):
            pair = values[k : k + 2]
            pair = pair if len(pair) == 2 else pair * 2
            put(flat, 8 * k, at, jnp.concatenate(pair, 0), 32)
        return carry

    lax.fori_loop(0, ROWS, row, 0, unroll=8)


def put_basis(own, other, own_k, other_k, potential, flat):
    def row(s, carry):
        at = lanes_at(s)
        for plane, (b, k) in enumerate(((own, own_k), (other, other_k))):
            beta, moved = flat_rows(b, s, PRJ), flat_rows(k, s, PRJ)
            put(flat, 2 * PRJ * plane, at, beta, 64)
            put(flat, 2 * PRJ * plane + PRJ, at, moved + potential[plane, pl.ds(s, 1)] * beta, 64)
        return carry

    lax.fori_loop(0, ROWS, row, 0, unroll=8)


def field_moments(fields_flat, basis_flat, count):
    both = products(fields_flat, basis_flat)
    both = both[:32] + both[32:]
    both = both + pltpu.roll(both, 64, 1)
    result = []
    for k in range(count):
        part = both[8 * k : 8 * k + 8]
        result.append(part + pltpu.roll(pltpu.roll(part, 96, 1), 4, 0))
    return result


def stack_rows(a, b):
    sub = lax.broadcasted_iota(jnp.int32, (8, LANES), 0)
    lane = lax.broadcasted_iota(jnp.int32, (8, LANES), 1)
    return jnp.where(lane < PRJ, jnp.where(sub < 4, a, pltpu.roll(b, 4, 0)), 0.0)


def early_moments_kernel(center, first, second, own, other, out, ahead_flat, fields_flat, basis_flat):
    put_fields((center, first, second), fields_flat)

    def row(s, carry):
        at = lanes_at(s)
        for plane, b in enumerate((own, other)):
            put(basis_flat, 2 * PRJ * plane, at, flat_rows(b, s, PRJ), 64)
        return carry

    for k in (16, 48, 80, 112):
        basis_flat[k : k + PRJ] = jnp.zeros((PRJ, ROWS * LANES), jnp.bfloat16)
    lax.fori_loop(0, ROWS, row, 0, unroll=8)
    found = field_moments(fields_flat, basis_flat, 3)
    out[...] = jnp.concatenate([stack_rows(found[0], found[1]), stack_rows(found[2], 0.0 * found[2])], 0)
    ahead_flat[0:16] = fields_flat[16:32]
    ahead_flat[16:32] = fields_flat[48:64]


def moments_kernel(known, ahead_flat, own, other, own_k, other_k, potential, gram, out, basis_flat):
    def row(s, carry):
        at = lanes_at(s)
        for plane, (b, k) in enumerate(((own, own_k), (other, other_k))):
            wide = flat_rows(k, s, PRJ) + potential[plane, pl.ds(s, 1)] * flat_rows(b, s, PRJ)
            put(basis_flat, PRJ * plane, at, wide, 32)
        return carry

    lax.fori_loop(0, ROWS, row, 0, unroll=8)
    both = products(ahead_flat, basis_flat)
    both = both[:8] + both[16:24]
    both = both[:, :32] + both[:, 32:]
    both = jnp.concatenate([both, jnp.zeros((8, LANES - 32), f32)], 1)
    wide = both + pltpu.roll(pltpu.roll(both, LANES - PRJ, 1), 4, 0)
    moments = jnp.concatenate([known[...][:8], known[...][8:] + stack_rows(0.0 * wide, wide)], 0)
    share(out, moments + gram[...])


def middle_moments_kernel(
    center, potential, own, other, own_k, other_k, wave_x, wave_y, wave_z, out
):
    kinds = [
        (center, None),
        (center, "wide"),
        (center, lambda plane, j, beta: beta * wave_x[plane, j // PRJ_ATOM, 0:1]),
        (center, lambda plane, j, beta: beta * wave_y[j // PRJ_ATOM]),
        (center, lambda plane, j, beta: beta * wave_z[j // PRJ_ATOM]),
    ]
    out[...] = project((own, other, own_k, other_k), potential, kinds, 24)


def basis_kernel(own, other, own_k, other_k, potential, out):
    put_basis(own, other, own_k, other_k, potential, out)


def second_kernel(
    near, far, center, potential, column, basis_flat, known, first, second, out, edge, work, fields_flat
):
    two_steps(near, far, center, potential, column, first, edge, second, work)
    put_fields([x.reshape(8 * ROWS, LANES) for x in (first, second)], fields_flat)
    found = [pltpu.roll(x, LANES - PRJ, 1) for x in field_moments(fields_flat, basis_flat, 2)]
    value = known[...]
    packed = value[:8] + pltpu.roll(stack_rows(*found), PRJ, 1)
    packed = packed + pltpu.roll(value[8:16], 2 * PRJ, 1) + pltpu.roll(value[16:], 3 * PRJ, 1)
    share(out, packed)


def times_i(x):
    row = lax.broadcasted_iota(jnp.int32, (8, LANES), 0)
    return jnp.where(row < 2, -pltpu.roll(x, 6, 0), pltpu.roll(x, 2, 0))


def coefficients(later, flags, received, strengths, gram):
    upper, sign = flags[0], flags[1]
    sums = []
    for core in range(2):
        acc = received[core]
        for k in range(core + 2, 16, 2):
            acc = acc + received[k]
        sums.append(acc)
    mine = jnp.where(upper > 0.5, sums[1], sums[0])
    if later:
        mine = jnp.concatenate([mine, pltpu.roll(mine, LANES - PRJ, 1)], 0)
    lane = lax.broadcasted_iota(jnp.int32, (PRJ, LANES), 1)
    valid = lane < PRJ
    if later:
        grams = gram[...]
    else:
        theirs = jnp.where(upper > 0.5, sums[0], sums[1])
        turned = jnp.where(
            (lane >= 48) & (lane < 64) | (lane >= 80),
            pltpu.roll(theirs, PRJ, 1),
            pltpu.roll(theirs, LANES - PRJ, 1),
        )
        grams = mine + jnp.where(lane < 32, theirs, turned)
        gram[...] = grams

    def block(k):
        return jnp.where(valid, pltpu.roll(grams, LANES - PRJ * (k + 1), 1), 0.0)

    g0 = block(0)
    g1, g2 = (block(2), block(4)) if later else (block(1), block(3))
    weight = strengths[...]

    def moment(k):
        rolled = mine if k == 0 else pltpu.roll(mine, PRJ - 4 * k, 0)
        return jnp.where(valid, rolled, 0.0)[:8]

    def apply(c, g):
        return jnp.dot(c[:, :PRJ], g, precision=highest, preferred_element_type=f32)

    c0 = weight * moment(0)
    c1 = weight * (moment(1) + apply(c0, g0))
    c2 = weight * (moment(2) + apply(c0, g1) + apply(c1, g0))
    c3 = weight * (moment(3) + apply(c0, g2) + apply(c1, g1) + apply(c2, g0))
    e0 = times_i((sign * half_step) * c0 + (sign * A3) * c2) + A2 * c1 + A4 * c3
    e1 = A2 * c0 + A4 * c2
    return c0, c1, e0, e1


def spread_table(table, sets):
    row = lax.broadcasted_iota(jnp.int32, (PRJ, LANES), 0)
    lane = lax.broadcasted_iota(jnp.int32, (PRJ, LANES), 1)
    for k, c in enumerate(sets):
        for q in range(4):
            wide = jnp.broadcast_to(c[q : q + 1], (PRJ, LANES))
            column = jnp.sum(jnp.where(row == lane, wide, 0.0), axis=1, keepdims=True)
            for j in range(PRJ):
                table[j, k, q] = jnp.broadcast_to(column[j : j + 1], (8, LANES))


def combine(out, start, basis, potential, table):
    def tile(i, carry):
        rows = pl.ds(pl.multiple_of(i * 8, 8), 8)
        totals = [start(plane, rows) for plane in range(2)]
        v = [potential[plane, rows] for plane in range(2)]
        for j in range(PRJ):
            by_wide = [table[j, 0, q] for q in range(4)]
            by_beta = [table[j, 1, q] for q in range(4)]
            for plane, total in enumerate(totals):
                beta = basis[plane][j, rows]
                wide = basis[2 + plane][j, rows] + v[plane] * beta
                for q in range(4):
                    total[q] = total[q] + by_wide[q] * wide + by_beta[q] * beta
        for plane, total in enumerate(totals):
            for q in range(4):
                out[plane, q, rows] = total[q]
        return carry

    lax.fori_loop(0, ROWS // 8, tile, 0)


def advance_kernel(later, flags, received, strengths, second, own, other, own_k, other_k, potential, *refs):
    if later:
        gram, out, rest, table = refs
    else:
        out, rest, gram, table = refs
    c0, c1, e0, e1 = coefficients(later, flags, received, strengths, gram)
    rest[0] = e1
    rest[1] = e0
    spread_table(table, (c0, c1))

    def start(plane, rows):
        return [second[plane, q, rows] for q in range(4)]

    combine(out, start, (own, other, own_k, other_k), potential, table)


def partial_kernel(flags, center, first, second, own, other, own_k, other_k, potential, rest, out, table):
    sign = flags[1]
    spread_table(table, (rest[0], rest[1]))

    def start(plane, rows):
        moved = [first[plane, q, rows] for q in range(4)]
        mixed = [-moved[2], -moved[3], moved[0], moved[1]]
        return [
            center[plane, q, rows] + (sign * half_step) * mixed[q] + A2 * second[plane, q, rows]
            for q in range(4)
        ]

    combine(out, start, (own, other, own_k, other_k), potential, table)


def last_kernel(flags, near, far, center, potential, column, partial, out, first, edge, second, work):
    two_steps(near, far, center, potential, column, first, edge, second, work)
    sign = flags[1]
    for plane in range(2):
        for q in range(4):
            mixed = -first[plane, q + 2] if q < 2 else first[plane, q - 2]
            out[plane, q] = partial[plane, q] + (sign * A3) * mixed + A4 * second[plane, q]


def payload_kernel(flags, mine, yours, received, strengths, out):
    turned = [mine[0, q] * yours[q + 2] - mine[0, q + 2] * yours[q] for q in range(2)]
    density = (-2.0 * half_step * flags[1]) * (turned[0] + turned[1])
    sums = []
    for core in range(2):
        acc = received[core]
        for k in range(core + 2, 16, 2):
            acc = acc + received[k]
        sums.append(acc)
    forces = []
    for q in range(3):
        rows, shift = slice(4 * (q % 2), 4 * (q % 2) + 4), LANES - (2 + q // 2) * PRJ
        slopes = [pltpu.roll(x, shift, 1)[rows] for x in sums]
        products = sums[0][:4] * slopes[1] + sums[1][:4] * slopes[0]
        forces.append(strengths[...] * jnp.sum(products, axis=0, keepdims=True))
    for k in range(16):
        first = 9 * k // 2
        out[k] = jnp.concatenate([density[first : first + 5]] + forces, 0)


def outcome_kernel(odd, received, density, forces):
    total = received[0]
    for k in range(1, 16):
        total = total + received[k]
    lane = lax.broadcasted_iota(jnp.int32, (1, LANES), 1)
    moved = pltpu.roll(total, 64, 1)
    for k in range(5):
        start = total[k : k + 1]
        shifted = jnp.where(lane < 64, moved[k : k + 1], moved[min(k + 1, 4) : min(k + 1, 4) + 1])
        row = jnp.where(odd[0] > 0, shifted, start)
        width = min(LANES, 576 - k * LANES)
        density[:, k * LANES : k * LANES + width] = row[:, :width]
    atom = lax.broadcasted_iota(jnp.int32, (3, LANES), 1) // PRJ_ATOM
    column = lax.broadcasted_iota(jnp.int32, (3, 4), 1)
    result = jnp.zeros((3, 4), f32)
    for a in range(4):
        part = jnp.sum(jnp.where(atom == a, total[5:8], 0.0), axis=1, keepdims=True)
        result = jnp.where(column == a, part * (1.0 / NB), result)
    forces[...] = result


def swap_core(x):
    return lax.ppermute(x, "space", [(i, i ^ 1) for i in range(16)])


def fence(*values):
    return lax.optimization_barrier(values)


def body(
    psi_start,
    adjoint_end,
    potential_now,
    potential_next,
    projector_tiles,
    tile_map,
    strengths,
    positions,
):
    space, band = lax.axis_index("space"), lax.axis_index("band")
    lower = (space % 2) == 0
    column = jnp.asarray(columns())
    plane_shape = (ROWS, LANES)
    fields_shape = (2, 4) + plane_shape
    rows_shape = (PRJ,) + plane_shape
    flags = jnp.stack([jnp.where(lower, 0.0, 1.0), jnp.where(lower, -1.0, 1.0)]).astype(f32)
    atom = (band // PRJ_ATOM).astype(jnp.int32).reshape(1)
    odd = (band % 2).astype(jnp.int32).reshape(1)

    far_memory = pl.BlockSpec(memory_space=pltpu.HBM)
    payload = pl.pallas_call(
        mask_kernel,
        out_shape=jax.ShapeDtypeStruct(rows_shape, f32),
        in_specs=[SMEM, far_memory, far_memory],
        out_specs=VMEM,
        scratch_shapes=[
            pltpu.VMEM(plane_shape, f32),
            pltpu.VMEM((4, ROWS), jnp.int32),
            pltpu.SemaphoreType.DMA((2,)),
        ],
        compiler_params=params(60),
    )(atom, projector_tiles.reshape(plane_shape), tile_map.reshape(4, ROWS))
    basis_own = lax.all_to_all(payload, "band", 0, 0, tiled=True)

    kept, given, own = call(
        give_kernel,
        [(4,) + plane_shape, (6,) + plane_shape, (2,) + plane_shape],
        [
            flags,
            psi_start.reshape((4,) + plane_shape),
            adjoint_end.reshape((4,) + plane_shape),
            potential_now.reshape(plane_shape),
            potential_next.reshape(plane_shape),
        ],
        scalars=1,
    )
    other = swap_core(given)
    near_message, far_message, center = call(
        pack_kernel,
        [(10,) + plane_shape, (10,) + plane_shape, fields_shape],
        [kept, own, other],
    )

    from_near = [(i, (i + 2) % 16 if i % 2 == 0 else (i - 2) % 16) for i in range(16)]
    from_far = [(j, i) for i, j in from_near]
    beside = [(i, (i + 1) % 16 if i % 2 else (i - 1) % 16) for i in range(16)]

    def exchange(fields):
        flat = fields.reshape((8,) + plane_shape)
        return (lax.ppermute(flat, "space", from_near), lax.ppermute(flat, "space", from_far))

    near = lax.ppermute(near_message, "space", from_near)
    far = lax.ppermute(far_message, "space", from_far)

    basis_own, near, far, strengths, positions = fence(
        basis_own, near, far, strengths, positions
    )
    basis_near = lax.ppermute(basis_own, "space", beside)
    basis_other = swap_core(basis_own)

    field_scratch = pltpu.VMEM(fields_shape, f32)
    work_scratch = pltpu.VMEM((4, 3) + plane_shape, f32)
    first, second, early, late = call(
        start_kernel,
        [fields_shape, fields_shape, (4,) + plane_shape, (4,) + plane_shape],
        [flags, near, far, center, own, other, column],
        scratch=[field_scratch, work_scratch],
        scalars=1,
    )
    flat_shape = (PRJ * ROWS, LANES)
    fields_flat = (8 * ROWS, LANES)
    known, ahead_flat = call(
        early_moments_kernel,
        [(16, LANES), jax.ShapeDtypeStruct((32, ROWS * LANES), jnp.bfloat16)],
        [x.reshape(fields_flat) for x in (center, first, second)]
        + [x.reshape(flat_shape) for x in (basis_own, basis_other)],
        scratch=[
            pltpu.VMEM((64, ROWS * LANES), jnp.bfloat16),
            pltpu.VMEM((128, ROWS * LANES), jnp.bfloat16),
        ],
        mib=12,
    )
    basis_near, first, second, early, late, known = fence(
        basis_near, first, second, early, late, known
    )
    kinetic_own = call(
        kinetic_kernel,
        rows_shape,
        [basis_own, basis_other, basis_near, column],
        scratch=[work_scratch],
    )
    kinetic_other = swap_core(kinetic_own)
    gram_part = call(
        gram_kernel,
        (PRJ, LANES),
        [basis_own.reshape(flat_shape), kinetic_own.reshape(flat_shape), early, late],
        scratch=[pltpu.VMEM((128, ROWS * LANES), jnp.bfloat16)],
        mib=12,
    )
    kinetic_other, gram_part = fence(kinetic_other, gram_part)
    basis = [basis_own, basis_other, kinetic_own, kinetic_other]
    part = call(
        moments_kernel,
        (16, 16, LANES),
        [known, ahead_flat] + [x.reshape(flat_shape) for x in basis] + [early, gram_part],
        scratch=[pltpu.VMEM((64, ROWS * LANES), jnp.bfloat16)],
        mib=12,
    )

    table_scratch = pltpu.VMEM((PRJ, 2, 4, 8, LANES), f32)
    rest_shape = (2, 8, LANES)
    received = lax.all_to_all(part, "space", 0, 0, tiled=True)
    received, strengths, positions, space, first, second, early, late, center = fence(
        received, strengths, positions, space, first, second, early, late, center
    )
    plane = space + jnp.stack([jnp.int32(0), 1 - 2 * (space % 2)])
    flat = np.arange(ROWS * LANES, dtype=np.int32)
    wave_x = jnp.sin(
        2.0 * math.pi / 16 * (plane[:, None] - positions[0][None, :]).astype(f32)
    )
    wave_x = jnp.broadcast_to(wave_x[:, :, None, None], (2, 4, 8, LANES))
    wave_y = jnp.sin(
        2.0 * math.pi / NY * (jnp.asarray(flat // NZ)[None, :] - positions[1][:, None]).astype(f32)
    ).reshape((4,) + plane_shape)
    wave_z = jnp.sin(
        2.0 * math.pi / NZ * (jnp.asarray(flat % NZ)[None, :] - positions[2][:, None]).astype(f32)
    ).reshape((4,) + plane_shape)
    weight = jnp.pad(strengths, (0, LANES - PRJ)).reshape(1, LANES)
    u2, rest, gram = call(
        functools.partial(advance_kernel, False),
        [fields_shape, rest_shape, (PRJ, LANES)],
        [flags, received, weight, second] + basis + [early],
        scratch=[table_scratch],
        scalars=1,
    )

    def finish(center, first, second, around, u2, rest, parts=None):
        flat = u2.reshape((8,) + plane_shape)
        near = lax.ppermute(flat, "space", from_near)
        shared = None
        if parts is not None:
            flat, parts = fence(flat, parts)
            far = lax.ppermute(flat, "space", from_far)
            shared = lax.all_to_all(parts, "band", 0, 0, tiled=True)
            rest, shared = fence(rest, shared)
        partial = call(
            partial_kernel,
            fields_shape,
            [flags, center, first, second] + basis + [around, rest],
            scratch=[table_scratch],
            scalars=1,
        )
        if parts is None:
            flat, partial = fence(flat, partial)
            far = lax.ppermute(flat, "space", from_far)
        return shared, call(
            last_kernel,
            fields_shape,
            [flags, near, far, u2, around, column, partial],
            scratch=[field_scratch] * 3 + [work_scratch],
            scalars=1,
        )

    _, mid = finish(center, first, second, early, u2, rest)
    flat = mid.reshape((8,) + plane_shape)
    near = lax.ppermute(flat, "space", from_near)
    flat, late = fence(flat, late)
    basis_flat = call(
        basis_kernel,
        jax.ShapeDtypeStruct((128, ROWS * LANES), jnp.bfloat16),
        [x.reshape(flat_shape) for x in basis] + [late],
    )
    flat, basis_flat = fence(flat, basis_flat)
    far = lax.ppermute(flat, "space", from_far)
    yours = swap_core(mid[1])
    known = call(
        middle_moments_kernel,
        (24, LANES),
        [mid, late] + basis + [wave_x, wave_y, wave_z],
    )
    first, second, part = call(
        second_kernel,
        [fields_shape, fields_shape, (16, 8, LANES)],
        [near, far, mid, late, column, basis_flat, known],
        scratch=[
            field_scratch,
            work_scratch,
            pltpu.VMEM((64, ROWS * LANES), jnp.bfloat16),
        ],
    )
    part, yours = fence(part, yours)
    received = lax.all_to_all(part, "space", 0, 0, tiled=True)
    received, first, second, late, mid, yours = fence(received, first, second, late, mid, yours)
    u2, rest = call(
        functools.partial(advance_kernel, True),
        [fields_shape, rest_shape],
        [flags, received, weight, second] + basis + [late, gram],
        scratch=[table_scratch],
        scalars=1,
    )

    u2, yours = fence(u2, yours)
    parts = call(
        payload_kernel, (16, 8, LANES), [flags, mid, yours, received, weight], scalars=1
    )
    shared, end = finish(mid, first, second, late, u2, rest, parts)
    density, forces = call(outcome_kernel, [(1, 576), (3, 4)], [odd, shared], scalars=1)

    swapped = swap_core(end[1])
    psi_end = jnp.where(lower, end[0], swapped).reshape(psi_start.shape)
    adjoint_start = jnp.where(lower, swapped, end[0]).reshape(adjoint_end.shape)
    return (psi_end, adjoint_start, density, forces)


def solution(mesh):
    return jax.shard_map(
        body,
        mesh=mesh,
        in_specs=(
            P(None, "band", "space", None),
            P(None, "band", "space", None),
            P("space", None),
            P("space", None),
            P("band", "space", None),
            P(None, "space", None),
            P(),
            P(),
        ),
        out_specs=(
            P(None, "band", "space", None),
            P(None, "band", "space", None),
            P("space", "band"),
            P(),
        ),
        check_vma=False,
    )
```
